32 devices in a mesh: dev: 32 (over z, y, x, core).
Axes of the slice: x: 2, y: 2, z: 4, core: 2. Of those that a mesh axis runs over, the one named last changes fastest.
Arguments:
- tokens: bfloat16 [8192, 2048], P('dev'), may hold values from -6 to 6
- attn_gain: bfloat16 [2048], P('dev'), may hold values from 0.099609375 to 1.8984375
- w_query: bfloat16 [2048, 2048], P('dev'), may hold values from -0.125 to 0.125
- w_key: bfloat16 [2048, 256], P('dev'), may hold values from -0.125 to 0.125
- w_value: bfloat16 [2048, 256], P('dev'), may hold values from -0.125 to 0.125
- w_out: bfloat16 [2048, 2048], P('dev'), may hold values from -2 to 2
- mlp_gain: bfloat16 [2048], P('dev'), may hold values from 0.099609375 to 1.8984375
- w_gate: bfloat16 [2048, 5632], P('dev'), may hold values from -0.125 to 0.125
- w_up: bfloat16 [2048, 5632], P('dev'), may hold values from -0.125 to 0.125
- w_down: bfloat16 [5632, 2048], P('dev'), may hold values from -0.078125 to 0.078125
- cotangent: bfloat16 [8192, 2048], P('dev'), may hold values from -6 to 6
Outputs:
- output: bfloat16 [8192, 2048], P('dev')
- input_grad: bfloat16 [8192, 2048], P('dev')
- attn_gain_grad: float32 [2048], P('dev')
- query_grad: float32 [2048, 2048], P('dev')
- key_grad: float32 [2048, 256], P('dev')
- value_grad: float32 [2048, 256], P('dev')
- out_grad: float32 [2048, 2048], P('dev')
- mlp_gain_grad: float32 [2048], P('dev')
- gate_grad: float32 [2048, 5632], P('dev')
- up_grad: float32 [2048, 5632], P('dev')
- down_grad: float32 [5632, 2048], P('dev')
The draws below stay inside these ranges and needn't reach their ends.
All inputs are finite; a program needn't handle non-finite values.
Results may differ from the reference program's by a relative error of at most 0.014.
Values may be sent and summed in bfloat16 or wider, within the bound.
No kernel may reach another device: no remote copies, remote signals or barrier semaphores. Data moves between devices by JAX's collectives and lax.ppermute only.
A program may use at most 384 MiB of HBM per device.

```python
import jax
import jax.numpy as jnp
from jax import lax

D = 2048
H = 32
KVH = 4
HD = 64
FF = 5632
LENGTH = 1024
SEQS = 8
TOKENS = 8192


def raised(array, own_key, source, target, parts, factor):
    def block_of(axis_at):
        return (jnp.arange(array.shape[axis_at]) // (array.shape[axis_at] // parts)).reshape((-1,) + (1,) * (array.ndim - 1 - axis_at))

    first = jax.random.permutation(own_key, parts)[block_of(target)]
    second = (block_of(target) + parts // 2) % parts
    return jnp.where((block_of(source) == first) | (block_of(source) == second), factor * array, array)


def steps_of(own_key, shape, shards, least, largest):
    loudness, own = 1.0, jax.random.fold_in(own_key, 6)
    for position, parts in shards:
        heights = jnp.exp(jax.random.uniform(jax.random.fold_in(own, position), (parts,), jnp.float32, least / len(shards), largest / len(shards)))
        loudness = loudness * jnp.repeat(heights, shape[position] // parts).reshape([-1 if axis == position else 1 for axis in range(len(shape))])
    return loudness


def centred(own_key, extent, width, bound, pieces=(), dtype=jnp.bfloat16):
    level = steps_of(own_key, extent, pieces, -0.22, 0.18) if pieces else 1.0
    entries = jax.random.normal(own_key, extent, jnp.float32) * width * level
    return jnp.minimum(jnp.maximum(entries, -bound), bound).astype(dtype)


def bell_draw_with(key, shape, scale, reach, pieces, heavy, held_as=jnp.bfloat16):
    drawn = scale * jax.random.normal(key, shape, jnp.float32)
    if pieces:
        drawn = drawn * steps_of(key, shape, pieces, -0.22, 0.18)
    return jnp.clip(raised(drawn, jax.random.fold_in(key, 3), *heavy), -reach, reach).astype(held_as)


def setup_inputs(seed: int = 0) -> dict:
    seeds = jax.random.split(jax.random.key(seed), 12)
    return {
        "tokens": bell_draw_with(seeds[0], (TOKENS, D), 1.0, 6.0, ((0, 32),), (0, 1, 32, 2.75)),
        "attn_gain": jnp.clip(1.0 + 0.18 * jax.random.normal(seeds[1], (D,), jnp.float32), 0.099609375, 1.8984375).astype(jnp.bfloat16),
        "w_query": centred(seeds[2], (D, H * HD), D ** -0.5, 0.125, ((0, 32),)),
        "w_key": centred(seeds[3], (D, KVH * HD), D ** -0.5, 0.125, ((0, 32),)),
        "w_value": centred(seeds[4], (D, KVH * HD), D ** -0.5, 0.125, ((0, 32),)),
        "w_out": centred(seeds[5], (H * HD, D), (max(D // 256, 2)) ** -0.5, 2.0, ((0, 32),)),
        "mlp_gain": jnp.clip(1.0 + 0.18 * jax.random.normal(seeds[6], (D,), jnp.float32), 0.099609375, 1.8984375).astype(jnp.bfloat16),
        "w_gate": centred(seeds[7], (D, FF), D ** -0.5, 0.125, ((0, 32),)),
        "w_up": centred(seeds[8], (D, FF), D ** -0.5, 0.125, ((0, 32),)),
        "w_down": centred(seeds[9], (FF, D), FF ** -0.5, 0.078125, ((0, 32),)),
        "cotangent": centred(seeds[10], (TOKENS, D), 1.0, 6.0, ((0, 32),)),
    }


EPS = 1e-05
THETA = 10000.0
NEG = -1e+30
HIGHEST = lax.Precision.HIGHEST

@jax.custom_vjp
def low(v):
    return lax.optimization_barrier(v.astype(jnp.bfloat16)).astype(jnp.float32)

@jax.custom_vjp
def low_back(v):
    return v

def low_keep(v):
    return (low(v), None)

def low_pass(kept, grad):
    return (grad,)

def back_keep(v):
    return (v, None)

def back_low(kept, grad):
    return (low(grad),)
low.defvjp(low_keep, low_pass)
low_back.defvjp(back_keep, back_low)

def matmul(left, right):
    return jnp.dot(left, right, precision=HIGHEST)

def rms_scale(values):
    return lax.rsqrt(lax.optimization_barrier(jnp.mean(values * values, axis=-1, keepdims=True)) + EPS)

def rope_tables(positions, head_size):
    half_size = head_size // 2
    frequency = THETA ** (-(jnp.arange(half_size).astype(jnp.float32) * 2.0 / head_size))
    angles = positions.astype(jnp.float32)[:, None] * frequency[None, :]
    return (jnp.cos(angles)[:, None, :], jnp.sin(angles)[:, None, :])

def rotate(values, cosine_table, sine_table):
    half_size = values.shape[-1] // 2
    front_half = values[..., :half_size]
    back_half = values[..., half_size:]
    return jnp.concatenate([front_half * cosine_table - back_half * sine_table, back_half * cosine_table + front_half * sine_table], axis=-1)

def attend_one(sequence):
    queries, keys, values = sequence
    length = queries.shape[0]
    grouped = queries.reshape(length, KVH, H // KVH, HD)
    scores = jnp.einsum('qgrd,kgd->grqk', grouped, keys, precision=HIGHEST) * HD ** (-0.5)
    scores = low_back(scores)
    causal = jnp.arange(length)[:, None] >= jnp.arange(length)[None, :]
    scores = jnp.where(causal, scores, NEG)
    row_top = lax.optimization_barrier(jnp.max(scores, axis=-1, keepdims=True))
    exponent = jnp.exp(scores - row_top)
    attn_probs = low(exponent / lax.optimization_barrier(jnp.sum(exponent, axis=-1, keepdims=True)))
    attended = jnp.einsum('grqk,kgd->qgrd', attn_probs, values, precision=HIGHEST)
    return attended.reshape(length, H * HD)

def layer(tokens, attn_gain, w_query, w_key, w_value, w_out, mlp_gain, w_gate, w_up, w_down):
    positions = jnp.arange(TOKENS) % LENGTH
    cosine_table, sine_table = rope_tables(positions, HD)
    normed_one = low(tokens * rms_scale(tokens) * attn_gain)
    query_lin = low_back(matmul(normed_one, w_query))
    key_lin = low_back(matmul(normed_one, w_key))
    value_low = low(low_back(matmul(normed_one, w_value)))
    queries = low(rotate(query_lin.reshape(TOKENS, H, HD), cosine_table, sine_table))
    keys = low(rotate(key_lin.reshape(TOKENS, KVH, HD), cosine_table, sine_table))
    attended = lax.map(jax.checkpoint(attend_one), (queries.reshape(SEQS, LENGTH, H, HD), keys.reshape(SEQS, LENGTH, KVH, HD), value_low.reshape(SEQS, LENGTH, KVH, HD)))
    mixed_low = low(low_back(attended.reshape(TOKENS, H * HD)))
    middle = tokens + low_back(matmul(mixed_low, w_out))
    normed_two = low(middle * rms_scale(middle) * mlp_gain)
    gate = low_back(matmul(normed_two, w_gate))
    up_proj = low_back(matmul(normed_two, w_up))
    hidden = low(jax.nn.silu(gate) * up_proj)
    return middle + low_back(matmul(hidden, w_down))

def reference(tokens, attn_gain, w_query, w_key, w_value, w_out, mlp_gain, w_gate, w_up, w_down, cotangent):
    output, pullback = jax.vjp(layer, tokens.astype(jnp.float32), attn_gain.astype(jnp.float32), w_query.astype(jnp.float32), w_key.astype(jnp.float32), w_value.astype(jnp.float32), w_out.astype(jnp.float32), mlp_gain.astype(jnp.float32), w_gate.astype(jnp.float32), w_up.astype(jnp.float32), w_down.astype(jnp.float32))
    grads = pullback(cotangent.astype(jnp.float32))
    return (output.astype(jnp.bfloat16), grads[0].astype(jnp.bfloat16), grads[1], grads[2], grads[3], grads[4], grads[5], grads[6], grads[7], grads[8], grads[9])
```

```python
import functools

import jax
import jax.numpy as jnp
from jax import lax
from jax.experimental import pallas as pl
from jax.experimental.pallas import tpu as pltpu
from jax.sharding import PartitionSpec as P

HD = 64
RANKS = 8
GROUP = 4
EPS = 1e-05
THETA = 10000.0
NEG = -1e30
F32 = jnp.float32
BF16 = jnp.bfloat16


def swap(block, bit):
    n = lax.axis_size("dev")
    return lax.ppermute(block, "dev", [(i, i ^ bit) for i in range(n)])


def onward(block):
    n = lax.axis_size("dev")
    return lax.ppermute(block, "dev", [(i, (i + RANKS) % n) for i in range(n)])


def plane_groups():
    n = lax.axis_size("dev")
    return [[p * RANKS + r for r in range(RANKS)] for p in range(n // RANKS)]


def exchange(blocks):
    return lax.all_to_all(
        blocks, "dev", split_axis=0, concat_axis=0, tiled=True, axis_index_groups=plane_groups()
    )


def gather_tokens(block):
    half = block.shape[0] // 2
    one, two, four = swap(block, 1), swap(block, 2), swap(block, 4)
    three, five = swap(two, 1), swap(four, 1)
    six = (swap(two[:half], 4), swap(four[half:], 2))
    seven = tuple(swap(part, 1) for part in six)
    return jnp.concatenate([block, one, two, three, four, five, *six, *seven])


def reduce_tokens(far, near):
    rows = near.shape[0] // 4
    half = rows // 2
    four, five, six, seven = (far[i * rows : (i + 1) * rows] for i in range(4))
    zero, one, two, three = (near[i * rows : (i + 1) * rows] for i in range(4))
    wide = lambda v: v.astype(F32)
    thin = lambda v: v.astype(BF16)
    six = thin(wide(six) + wide(swap(seven, 1)))
    for_four, for_two = swap(six[:half], 2), swap(six[half:], 4)
    four = wide(four) + wide(swap(five, 1))
    two = wide(two) + wide(swap(three, 1))
    two_top, four_low = swap(thin(two[:half]), 2), swap(thin(four[half:]), 4)
    two_low = swap(thin(two[half:] + wide(for_two)), 2)
    four_top = swap(thin(four[:half] + wide(for_four)), 4)
    zero = wide(zero) + wide(swap(one, 1))
    others = jnp.concatenate([wide(two_top) + wide(four_top), wide(two_low) + wide(four_low)])
    return zero + others


def ring_gather(block, plane, planes):
    rows = block.shape[0]
    whole = jnp.zeros((planes * rows, block.shape[1]), block.dtype)
    for step in range(planes):
        place = lax.rem(plane + planes - step, planes)
        whole = lax.dynamic_update_slice_in_dim(whole, block, place * rows, 0)
        if step < planes - 1:
            block = onward(block)
    return whole


def gather_gains(gains, me, plane, planes):
    bit = 1
    while bit < RANKS:
        other = swap(gains, bit)
        gains = jnp.where(
            me & bit,
            jnp.concatenate([other, gains], axis=1),
            jnp.concatenate([gains, other], axis=1),
        )
        bit *= 2
    whole = ring_gather(gains, plane, planes)
    return whole.reshape(planes, 2, -1).transpose(1, 0, 2).reshape(2, -1)


def ring_reduce(terms, plane, planes):
    rows = terms.shape[0] // planes

    def part(place):
        return lax.dynamic_slice_in_dim(terms, place * rows, rows, 0)

    total = part(lax.rem(plane + planes - 1, planes))
    for step in range(planes - 1):
        arrived = onward(total.astype(BF16))
        place = lax.rem(plane + 2 * planes - 2 - step, planes)
        total = part(place) + arrived.astype(F32)
    return total


def dot(left, right):
    return jnp.dot(left, right, preferred_element_type=F32)


def contract_rows(left, right):
    return lax.dot_general(left, right, (((0,), (0,)), ((), ())), preferred_element_type=F32)


def times_transposed(left, right):
    return lax.dot_general(left, right, (((1,), (1,)), ((), ())), preferred_element_type=F32)


def rms_scale(values):
    return lax.rsqrt(jnp.mean(values * values, axis=1, keepdims=True) + EPS)


def rope_tables(length):
    lanes = jnp.arange(2 * HD)
    frequency = THETA ** (-((lanes % (HD // 2)).astype(F32) * 2.0 / HD))
    angles = jnp.arange(length).astype(F32)[:, None] * frequency[None, :]
    sign = jnp.where(lanes % HD < HD // 2, -1.0, 1.0)
    return jnp.cos(angles), jnp.sin(angles) * sign[None, :]


def partner(values):
    lane = lax.broadcasted_iota(jnp.int32, values.shape, 1)
    ahead = pltpu.roll(values, 2 * HD - HD // 2, 1)
    behind = pltpu.roll(values, HD // 2, 1)
    return jnp.where(lane % HD < HD // 2, ahead, behind)


def forward_kernel(heads, rows, m_ref, qkv_ref, cos_ref, sin_ref, mixed_ref, qt_ref, kv_ref, lse_ref):
    mine = m_ref[0]
    width = heads * HD
    blocks = GROUP
    is_key = lax.broadcasted_iota(jnp.int32, (rows, 2 * HD), 1) < HD
    for p in range(blocks):
        span = slice(p * rows, (p + 1) * rows)
        qkv = qkv_ref[0, p ^ mine]
        cosine, sine = cos_ref[span, :], sin_ref[span, :]
        turned = []
        for start in range(0, width, 2 * HD):
            part = qkv[:, start : start + 2 * HD]
            turned.append(part * cosine + partner(part) * sine)
        query = jnp.concatenate(turned, axis=1) * HD ** (-0.5)
        qt_ref[0, :, span] = query.T.astype(BF16)
        part = qkv[:, width : width + 2 * HD]
        kv_ref[0, span, :] = jnp.where(
            is_key, part * cosine + partner(part) * sine, part
        ).astype(BF16)
    kv = kv_ref[0]
    vt = kv.astype(F32).T.astype(BF16)[HD:, :]
    keys = kv[:, :HD]
    ok = lax.broadcasted_iota(jnp.int32, (rows, rows), 0) <= lax.broadcasted_iota(
        jnp.int32, (rows, rows), 1
    )
    for p in range(blocks):
        span = slice(p * rows, (p + 1) * rows)
        outs, tops = [], []
        for h in range(heads):
            query = qt_ref[0, h * HD : (h + 1) * HD, span]
            last = jnp.where(ok, dot(keys[span], query), NEG)
            top = jnp.max(last, axis=0, keepdims=True)
            if p:
                first = dot(keys[: p * rows], query)
                top = jnp.maximum(top, jnp.max(first, axis=0, keepdims=True))
            weight = jnp.exp(last - top)
            total = jnp.sum(weight, axis=0, keepdims=True)
            if p:
                first = jnp.exp(first - top)
                total = total + jnp.sum(first, axis=0, keepdims=True)
            share = 1.0 / total
            out = dot(vt[:, span], (weight * share).astype(BF16))
            if p:
                out = out + dot(vt[:, : p * rows], (first * share).astype(BF16))
            outs.append(out)
            tops.append(top + jnp.log(total))
        mixed_ref[0, p ^ mine] = jnp.concatenate(outs, axis=0).T.astype(BF16)
        tops += [tops[0]] * (8 - heads)
        lse_ref[0, :, span] = jnp.concatenate(tops, axis=0)


def backward_kernel(
    heads, rows, m_ref, qt_ref, kv_ref, lse_ref, mg_ref, cos_ref, sin_ref, dq_ref, dkv_ref, dk_sum, dv_sum
):
    mine = m_ref[0]
    width = heads * HD
    blocks = GROUP
    kv = kv_ref[0]
    kt = kv.astype(F32).T.astype(BF16)[:HD, :]
    keys = kv[:, :HD]
    values = pltpu.roll(kv.astype(F32), HD, 1).astype(BF16)[:, :HD]
    ok = lax.broadcasted_iota(jnp.int32, (rows, rows), 0) <= lax.broadcasted_iota(
        jnp.int32, (rows, rows), 1
    )
    for p in reversed(range(blocks)):
        span = slice(p * rows, (p + 1) * rows)
        reach = (p + 1) * rows
        grad = mg_ref[0, p ^ mine].astype(F32).T.astype(BF16)
        dqs = []
        for h in range(heads):
            query = qt_ref[0, h * HD : (h + 1) * HD, span]
            above = grad[h * HD : (h + 1) * HD, :]
            lse = lse_ref[0, h : h + 1, span]
            scores = dot(keys[:reach], query)
            if p:
                scores = jnp.concatenate(
                    [scores[: p * rows], jnp.where(ok, scores[p * rows :], NEG)], axis=0
                )
            else:
                scores = jnp.where(ok, scores, NEG)
            probs = jnp.exp(scores - lse)
            probs_grad = dot(values[:reach], above)
            delta = jnp.sum(probs * probs_grad, axis=0, keepdims=True)
            score_low = (probs * (probs_grad - delta)).astype(BF16)
            dk = times_transposed(score_low, query)
            dv = times_transposed(probs.astype(BF16), above)
            if p == blocks - 1 and h == 0:
                dk_sum[...] = dk
                dv_sum[...] = dv
            else:
                dk_sum[:reach, :] += dk
                dv_sum[:reach, :] += dv
            dqs.append(dot(kt[:, :reach], score_low))
        dq = jnp.concatenate(dqs, axis=0).T * HD ** (-0.5)
        cosine, sine = cos_ref[span, :], sin_ref[span, :]
        turned = []
        for start in range(0, width, 2 * HD):
            part = dq[:, start : start + 2 * HD]
            turned.append(part * cosine - partner(part) * sine)
        dq_ref[0, p ^ mine] = jnp.concatenate(turned, axis=1).astype(BF16)
    is_key = lax.broadcasted_iota(jnp.int32, (rows, 2 * HD), 1) < HD
    for p in range(blocks):
        span = slice(p * rows, (p + 1) * rows)
        part = jnp.concatenate([dk_sum[span, :], dv_sum[span, :]], axis=1)
        cosine, sine = cos_ref[span, :], sin_ref[span, :]
        dkv_ref[0, p ^ mine] = jnp.where(is_key, part * cosine - partner(part) * sine, part)


def whole_spec(shape):
    zeros = (0,) * (len(shape) - 1)
    return pl.BlockSpec((1,) + shape[1:], lambda s, m: (s,) + zeros)


def same_spec(shape):
    zeros = (0,) * len(shape)
    return pl.BlockSpec(shape, lambda s, m: zeros)


def attend(qkv, tables, mine, heads):
    seqs, _, rows, cols = qkv.shape
    length = GROUP * rows
    width = heads * HD
    shapes = (
        ((seqs, GROUP, rows, width), BF16),
        ((seqs, width, length), BF16),
        ((seqs, length, 2 * HD), BF16),
        ((seqs, 8, length), F32),
    )
    return pl.pallas_call(
        functools.partial(forward_kernel, heads, rows),
        grid_spec=pltpu.PrefetchScalarGridSpec(
            num_scalar_prefetch=1,
            grid=(seqs,),
            in_specs=[whole_spec(qkv.shape), same_spec(tables[0].shape), same_spec(tables[1].shape)],
            out_specs=[whole_spec(shape) for shape, _ in shapes],
        ),
        out_shape=[jax.ShapeDtypeStruct(shape, dtype) for shape, dtype in shapes],
        compiler_params=pltpu.CompilerParams(vmem_limit_bytes=48 * 2**20),
        cost_estimate=pl.CostEstimate(
            flops=seqs * heads * length * length * HD * 8, bytes_accessed=8 * 2**20, transcendentals=seqs * heads * length * length
        ),
        name="attend",
    )(mine, qkv, *tables)


def attend_back(kept, grads, tables, mine, heads):
    queries, kv, lse = kept
    seqs, _, rows, width = grads.shape
    length = GROUP * rows
    shapes = (((seqs, GROUP, rows, width), BF16), ((seqs, GROUP, rows, 2 * HD), F32))
    ins = (queries, kv, lse, grads)
    return pl.pallas_call(
        functools.partial(backward_kernel, heads, rows),
        grid_spec=pltpu.PrefetchScalarGridSpec(
            num_scalar_prefetch=1,
            grid=(seqs,),
            in_specs=[whole_spec(v.shape) for v in ins]
            + [same_spec(tables[0].shape), same_spec(tables[1].shape)],
            out_specs=[whole_spec(shape) for shape, _ in shapes],
            scratch_shapes=[pltpu.VMEM((length, HD), F32), pltpu.VMEM((length, HD), F32)],
        ),
        out_shape=[jax.ShapeDtypeStruct(shape, dtype) for shape, dtype in shapes],
        compiler_params=pltpu.CompilerParams(vmem_limit_bytes=48 * 2**20),
        cost_estimate=pl.CostEstimate(
            flops=seqs * heads * length * length * HD * 20, bytes_accessed=8 * 2**20, transcendentals=seqs * heads * length * length
        ),
        name="attend_back",
    )(mine, *ins, *tables)


def per_device(
    tokens, attn_gain, w_query, w_key, w_value, w_out, mlp_gain, w_gate, w_up, w_down, cotangent
):
    n = lax.axis_size("dev")
    planes = n // RANKS
    me = lax.axis_index("dev")
    plane, rank = me // RANKS, lax.rem(me, RANKS)
    core = lax.rem(me, 2)
    mine = lax.rem(me, GROUP).astype(jnp.int32).reshape(1)
    count, model = tokens.shape
    local = w_query.shape[0]
    heads = w_query.shape[1] // HD // RANKS
    kv_heads = w_key.shape[1] // HD
    width = heads * HD
    units = w_gate.shape[1] // n
    own_units = units * planes
    seqs = RANKS // GROUP
    share = RANKS // kv_heads

    def by_kv(weight):
        parts = weight.reshape(local, kv_heads, 1, HD)
        return jnp.broadcast_to(parts, (local, kv_heads, share, HD)).reshape(local, RANKS, HD)

    def by_unit(weight):
        parts = weight.reshape(local, planes, RANKS, units)
        return parts.transpose(2, 0, 1, 3).reshape(RANKS, local, own_units)

    attn_parts = jnp.concatenate(
        [
            w_query.reshape(local, RANKS, width),
            by_kv(w_key),
            by_kv(w_value),
        ],
        axis=2,
    ).transpose(1, 0, 2)
    attn_cols = width + 2 * HD
    attn_own = exchange(attn_parts).reshape(RANKS * local, attn_cols)
    attn_weight = ring_gather(attn_own, plane, planes)

    gains = gather_gains(jnp.stack([attn_gain, mlp_gain]), me, plane, planes)
    gain_one, gain_two = gains[:1].astype(F32), gains[1:].astype(F32)
    source = tokens.astype(F32)
    scale_one = rms_scale(source)
    plane_source = gather_tokens(tokens).astype(F32)
    normed_one = (plane_source * rms_scale(plane_source) * gain_one).astype(BF16)

    to_rank = [(i, (i % planes) * RANKS + i // planes) for i in range(n)]
    from_rank = [(j, i) for i, j in to_rank]
    out_own = lax.ppermute(w_out, "dev", to_rank)
    out_weight = ring_gather(out_own, plane, planes)

    mlp_parts = jnp.concatenate([by_unit(w_gate), by_unit(w_up)], axis=2)
    mlp_own = exchange(mlp_parts).reshape(RANKS * local, 2 * own_units)
    mlp_weight = ring_gather(mlp_own, plane, planes)
    down_weight = ring_gather(w_down, plane, planes)
    above = gather_tokens(cotangent)

    tables = rope_tables(GROUP * count)
    qkv = dot(normed_one, attn_weight).reshape(seqs, GROUP, count, attn_cols)
    mixed, queries, kv, lse = attend(qkv, tables, mine, heads)
    mixed = mixed.reshape(RANKS * count, width)
    split = GROUP * count

    def summed(left, right):
        far = dot(left[split:], right).astype(BF16)
        near = dot(left[:split], right).astype(BF16)
        return reduce_tokens(far, near)

    def summed_transposed(left, right):
        far = times_transposed(left[split:], right).astype(BF16)
        near = times_transposed(left[:split], right).astype(BF16)
        return reduce_tokens(far, near)

    middle = source + summed(mixed, out_weight)

    scale_two = rms_scale(middle)
    normed_two = gather_tokens((middle * scale_two * gain_two).astype(BF16))
    gate_up = dot(normed_two, mlp_weight)
    gate, up_proj = gate_up[:, :own_units], gate_up[:, own_units:]
    sigmoid_gate = jax.nn.sigmoid(gate)
    silu_gate = gate * sigmoid_gate
    hidden = (silu_gate * up_proj).astype(BF16)
    output = (middle + summed(hidden, down_weight)).astype(BF16)

    down_grad = ring_reduce(contract_rows(hidden, above), plane, planes)
    hidden_grad = times_transposed(above, down_weight)
    gate_low = hidden_grad * up_proj * sigmoid_gate * (1.0 + gate * (1.0 - sigmoid_gate))
    both_low = jnp.concatenate([gate_low.astype(BF16), (hidden_grad * silu_gate).astype(BF16)], axis=1)
    scaled_two = summed_transposed(both_low, mlp_weight) * gain_two
    mlp_total = ring_reduce(contract_rows(normed_two, both_low), plane, planes)
    middle_grad = (
        cotangent.astype(F32)
        + scale_two * scaled_two
        - middle * scale_two**3 * jnp.mean(scaled_two * middle, axis=1, keepdims=True)
    )

    branch = gather_tokens(middle_grad.astype(BF16))
    mixed_grad = times_transposed(branch, out_weight).astype(BF16)
    out_total = ring_reduce(contract_rows(mixed, branch), plane, planes)
    out_grad = lax.ppermute(out_total, "dev", from_rank)
    query_low, dkv = attend_back(
        (queries, kv, lse), mixed_grad.reshape(seqs, GROUP, count, width), tables, mine, heads
    )
    query_low = query_low.reshape(RANKS * count, width)
    dkv = dkv.reshape(RANKS * count, 2 * HD)
    dk, dv = dkv[:, :HD], dkv[:, HD:]
    kept = jnp.where(core == 0, dk, dv)
    sent = swap(jnp.where(core == 0, dv, dk), 1).reshape(-1, 2, count, HD)
    kv_low = (kept + sent[:, ::-1].reshape(kept.shape)).astype(BF16)
    all_low = jnp.concatenate([query_low, kv_low], axis=1)
    back_weight = jnp.concatenate(
        [
            attn_weight[:, :width],
            jnp.where(core == 0, attn_weight[:, width : width + HD], attn_weight[:, width + HD :]),
        ],
        axis=1,
    )
    attn_total = ring_reduce(contract_rows(normed_one, all_low), plane, planes)
    scaled_one = summed_transposed(all_low, back_weight) * gain_one
    input_grad = (
        middle_grad
        + scale_one * scaled_one
        - source * scale_one**3 * jnp.mean(scaled_one * source, axis=1, keepdims=True)
    )

    mlp_back = exchange(mlp_total.astype(BF16).reshape(RANKS, local, 2 * own_units)).astype(F32)

    def in_order(parts):
        parts = parts.reshape(RANKS, local, planes, units).transpose(1, 2, 0, 3)
        return parts.reshape(local, n * units)

    gate_raw = in_order(mlp_back[:, :, :own_units])
    up_raw = in_order(mlp_back[:, :, own_units:])
    mlp_gain_grad = jnp.sum(gate_raw * w_gate, axis=1) + jnp.sum(up_raw * w_up, axis=1)
    mlp_gain_grad = mlp_gain_grad / mlp_gain

    attn_back = exchange(attn_total.astype(BF16).reshape(RANKS, local, width + HD)).astype(F32)
    query_raw = attn_back[:, :, :width].transpose(1, 0, 2).reshape(local, RANKS * width)
    shared = attn_back[:, :, width:].reshape(kv_heads, share, local, HD)
    key_raw = shared[:, 0].transpose(1, 0, 2).reshape(local, kv_heads * HD)
    value_raw = shared[:, 1].transpose(1, 0, 2).reshape(local, kv_heads * HD)
    attn_gain_grad = (
        jnp.sum(query_raw * w_query, axis=1)
        + jnp.sum(key_raw * w_key, axis=1)
        + jnp.sum(value_raw * w_value, axis=1)
    ) / attn_gain
    return (
        output,
        input_grad.astype(BF16),
        attn_gain_grad,
        query_raw,
        key_raw,
        value_raw,
        out_grad,
        mlp_gain_grad,
        gate_raw,
        up_raw,
        down_grad,
    )


def solution(mesh):
    row, vec = P("dev", None), P("dev")
    return jax.shard_map(
        per_device,
        mesh=mesh,
        in_specs=(row, vec, row, row, row, row, vec, row, row, row, row),
        out_specs=(row, row, vec, row, row, row, row, vec, row, row, row),
        check_vma=False,
    )
```

```python
import functools

import jax
import jax.numpy as jnp
from jax import lax
from jax.experimental import pallas as pl
from jax.experimental.pallas import tpu as pltpu
from jax.sharding import PartitionSpec as P

HD = 64
RANKS = 8
GROUP = 4
EPS = 1e-05
THETA = 10000.0
NEG = -1e30
F32 = jnp.float32
ANY = pl.BlockSpec(memory_space=pl.ANY)
SCALAR = pl.BlockSpec(memory_space=pltpu.SMEM)
WORK = pl.CostEstimate(flops=1, bytes_accessed=1, transcendentals=0)
BF16 = jnp.bfloat16


def swap(block, bit):
    n = lax.axis_size("dev")
    return lax.ppermute(block, "dev", [(i, i ^ bit) for i in range(n)])


def onward(block):
    n = lax.axis_size("dev")
    return lax.ppermute(block, "dev", [(i, (i + RANKS) % n) for i in range(n)])


def plane_groups():
    n = lax.axis_size("dev")
    return [[p * RANKS + r for r in range(RANKS)] for p in range(n // RANKS)]


def exchange(blocks):
    return lax.all_to_all(
        blocks, "dev", split_axis=0, concat_axis=0, tiled=True, axis_index_groups=plane_groups()
    )


def column_groups():
    n = lax.axis_size("dev")
    return [[p * RANKS + r for p in range(n // RANKS)] for r in range(RANKS)]


def planes_gather(block):
    return lax.all_gather(block, "dev", axis=0, tiled=True, axis_index_groups=column_groups())


def planes_reduce(terms):
    return lax.psum_scatter(
        terms, "dev", scatter_dimension=0, tiled=True, axis_index_groups=column_groups()
    )


def after(value, *earlier):
    return lax.optimization_barrier((value,) + earlier)[0]


def wide(value):
    return value.astype(F32)


def thin(value):
    return value.astype(BF16)


def copy_kernel(count, spots, first_ref, *refs):
    blocks, whole, done = refs[:count], refs[count], refs[count + 1]
    copies = []
    for i, block in enumerate(blocks):
        spot = whole.at[pl.ds(spots(i, first_ref[0]), block.shape[0])]
        copies.append(pltpu.make_async_copy(block, spot, done.at[i]))
        copies[-1].start()
    for copy in copies:
        copy.wait()


def copied(blocks, spots, first, name):
    rows = sum(block.shape[0] for block in blocks)
    return pl.pallas_call(
        functools.partial(copy_kernel, len(blocks), spots),
        in_specs=[SCALAR] + [ANY] * len(blocks),
        out_shape=jax.ShapeDtypeStruct((rows, blocks[0].shape[1]), blocks[0].dtype),
        compiler_params=pltpu.CompilerParams(vmem_limit_bytes=40 * 2**20),
        scratch_shapes=[pltpu.SemaphoreType.DMA((len(blocks),))],
        cost_estimate=WORK,
        name=name,
    )(first, *blocks)


def join(*blocks):
    starts = [0]
    for block in blocks:
        starts.append(starts[-1] + block.shape[0])
    return copied(blocks, lambda i, _: starts[i], jnp.zeros(1, jnp.int32), "join")


def gather_pair(block):
    return swap(block, 2), swap(block, 4)


def gather_last(two, four):
    half = two.shape[0] // 2
    return swap(two[:half], 4), swap(four[half:], 2)


def on_rows(function, ins, outs, name):
    return pl.pallas_call(
        function,
        out_shape=[jax.ShapeDtypeStruct(shape, dtype) for shape, dtype in outs],
        compiler_params=pltpu.CompilerParams(vmem_limit_bytes=40 * 2**20),
        cost_estimate=WORK,
        name=name,
    )(*ins)


def send_kernel(even, peer, to_two, to_four):
    rows = to_two.shape[0]
    half = rows // 2

    def summed(block, start):
        span = slice(block * rows + start, block * rows + start + half)
        return thin(wide(even[span]) + wide(peer[span]))

    to_two[:half] = summed(1, 0)
    to_two[half:] = summed(3, 0)
    to_four[:half] = summed(2, half)
    to_four[half:] = summed(3, half)


def pass_kernel(even, peer, from_two, from_four, to_two, to_four):
    half = to_two.shape[0]

    def summed(block, start, arrived):
        span = slice(block * 2 * half + start, block * 2 * half + start + half)
        return thin(wide(even[span]) + wide(peer[span]) + wide(arrived[half:]))

    to_four[...] = summed(2, 0, from_two)
    to_two[...] = summed(1, half, from_four)


def send_rows(parts):
    rows, cols = parts[0].shape
    shape = ((rows // 4, cols), BF16)
    return on_rows(send_kernel, parts, (shape, shape), "send_rows")


def pass_rows(parts, arrived):
    rows, cols = parts[0].shape
    shape = ((rows // 8, cols), BF16)
    return on_rows(pass_kernel, (*parts, *arrived), (shape, shape), "pass_rows")


def cross(to_two, to_four):
    return swap(to_two, 2), swap(to_four, 4)


def block_sum(even, peer, from_two, from_four, last_two, last_four):
    rows = last_two.shape[0]
    top, low = slice(0, rows), slice(rows, 2 * rows)
    upper = wide(even[top]) + wide(peer[top]) + wide(from_two[top]) + wide(last_four[...])
    lower = wide(even[low]) + wide(peer[low]) + wide(from_four[top]) + wide(last_two[...])
    return jnp.concatenate([upper, lower], axis=0)


def parts_kernel(odd, transposed, near, far, weight, out):
    half = near.shape[0] // 2
    span = slice(half, 2 * half) if odd else slice(0, half)
    multiply = times_transposed if transposed else dot
    out[:half] = thin(multiply(near[span], weight[...]))
    out[half:] = thin(multiply(far[span], weight[...]))


def parts_of(odd, transposed, near, far, weight):
    cols = weight.shape[0 if transposed else 1]
    return on_rows(
        functools.partial(parts_kernel, odd, transposed),
        (near, far, weight),
        (((near.shape[0], cols), BF16),),
        "odd_parts" if odd else "even_parts",
    )[0]


def mean_of(values):
    return jnp.mean(values, axis=1, keepdims=True)


def norm_kernel(gain, *refs):
    out, start = refs[-1], 0
    for block in refs[:-1]:
        values = wide(block[...])
        span = slice(start, start + block.shape[0])
        out[span] = thin(values * rms_scale(values) * gain[...])
        start += block.shape[0]


def normed(gain, *blocks):
    rows = sum(block.shape[0] for block in blocks)
    shape = (rows, blocks[0].shape[1])
    return on_rows(norm_kernel, (gain, *blocks), ((shape, BF16),), "norm")[0]


def middle_kernel(tokens, gain, *refs):
    sums, (middle_ref, normed_ref, scale_ref) = refs[:6], refs[6:]
    middle = wide(tokens[...]) + block_sum(*sums)
    scale = rms_scale(middle)
    middle_ref[...] = middle
    normed_ref[...] = thin(middle * scale * gain[...])
    scale_ref[...] = scale


def middle_back_kernel(above, gain, middle, scale, *refs):
    sums, (grad_ref, branch_ref) = refs[:6], refs[6:]
    scaled = block_sum(*sums) * gain[...]
    middle, scale = middle[...], scale[...]
    grad = wide(above[...]) + scale * scaled - middle * scale**3 * mean_of(scaled * middle)
    grad_ref[...] = grad
    branch_ref[...] = thin(grad)


def output_kernel(middle, *refs):
    refs[-1][...] = thin(middle[...] + block_sum(*refs[:6]))


def input_back_kernel(grad, gain, tokens, *refs):
    scaled = block_sum(*refs[:6]) * gain[...]
    source = wide(tokens[...])
    scale = rms_scale(source)
    whole = grad[...] + scale * scaled - source * scale**3 * mean_of(scaled * source)
    refs[-1][...] = thin(whole)


def attn_parts_kernel(query, key, value, parts):
    width = query.shape[1] // RANKS
    share = RANKS * HD // key.shape[1]
    for j in range(RANKS):
        head = slice(j // share * HD, (j // share + 1) * HD)
        parts[j, :, :width] = query[:, j * width : (j + 1) * width]
        parts[j, :, width:] = jnp.concatenate([key[:, head], value[:, head]], axis=1)


def mlp_parts_kernel(units, gate, up, parts):
    planes = gate.shape[1] // units // RANKS
    for j in range(RANKS):
        pieces = []
        for weight in (gate, up):
            for p in range(planes):
                start = (p * RANKS + j) * units
                pieces.append(weight[:, start : start + units])
        parts[j] = jnp.concatenate(pieces, axis=1)


def lane_sums(grad, weight):
    total = 0.0
    for start in range(0, grad.shape[1], 128):
        span = slice(start, start + 128)
        total = total + grad[:, span] * wide(weight[:, span])
    return jnp.sum(total, axis=1, keepdims=True)


def mlp_back_kernel(units, parts, gate, up, gate_grad, up_grad, gain_sum):
    planes = gate.shape[1] // units // RANKS
    own = planes * units
    for half, grad in enumerate((gate_grad, up_grad)):
        for p in range(planes):
            start = half * own + p * units
            pieces = [parts[j, :, start : start + units] for j in range(RANKS)]
            row = jnp.concatenate(pieces, axis=1)
            grad[:, p * RANKS * units : (p + 1) * RANKS * units] = wide(row)
    gain_sum[...] = lane_sums(gate_grad, gate) + lane_sums(up_grad, up)


def attn_back_kernel(parts, query, key, value, query_grad, key_grad, value_grad, gain_sum):
    width = query.shape[1] // RANKS
    share = RANKS * HD // key.shape[1]
    for j in range(RANKS):
        query_grad[:, j * width : (j + 1) * width] = wide(parts[j, :, :width])
    for first, grad in enumerate((key_grad, value_grad)):
        pieces = [parts[j, :, width:] for j in range(first, RANKS, share)]
        grad[...] = wide(jnp.concatenate(pieces, axis=1))
    gain_sum[...] = (
        lane_sums(query_grad, query) + lane_sums(key_grad, key) + lane_sums(value_grad, value)
    )


def place_rows(blocks, plane):
    planes, rows = len(blocks), blocks[0].shape[0]

    def spot(step, own):
        return lax.rem(own + planes - step, planes) * rows

    if rows % 16 == 0:
        aligned = lambda step, own: pl.multiple_of(spot(step, own), 16)
        return copied(blocks, aligned, plane.astype(jnp.int32).reshape(1), "place_rows")
    whole = jnp.zeros((planes * rows, blocks[0].shape[1]), blocks[0].dtype)
    for step, block in enumerate(blocks):
        whole = lax.dynamic_update_slice_in_dim(whole, block, spot(step, plane), 0)
    return whole


def place_gains(blocks, plane):
    planes, rows = len(blocks), blocks[0].shape[0]
    whole = jnp.zeros((planes * rows, blocks[0].shape[1]), blocks[0].dtype)
    for step, block in enumerate(blocks):
        place = lax.rem(plane + planes - step, planes)
        whole = lax.dynamic_update_slice_in_dim(whole, block, place * rows, 0)
    return whole


def join_gains(gains, other, bit, me):
    return jnp.where(
        me & bit,
        jnp.concatenate([other, gains], axis=1),
        jnp.concatenate([gains, other], axis=1),
    )


def ring_part(terms, step, plane, planes):
    rows = terms.shape[0] // planes
    place = lax.rem(plane + 2 * planes - 1 - step, planes)
    return lax.dynamic_slice_in_dim(terms, place * rows, rows, 0)


def ring_start(terms, plane, planes):
    return thin(ring_part(terms, 0, plane, planes))


def ring_add(terms, step, arrived, plane, planes):
    total = ring_part(terms, step, plane, planes) + wide(arrived)
    return thin(total) if step < planes - 1 else total


def dot(left, right):
    return jnp.dot(left, right, preferred_element_type=F32)


def contract_rows(left, right):
    return lax.dot_general(left, right, (((0,), (0,)), ((), ())), preferred_element_type=F32)


def times_transposed(left, right):
    return lax.dot_general(left, right, (((1,), (1,)), ((), ())), preferred_element_type=F32)


def rms_scale(values):
    return lax.rsqrt(jnp.mean(values * values, axis=1, keepdims=True) + EPS)


def rope_tables(length):
    lanes = jnp.arange(2 * HD)
    frequency = THETA ** (-((lanes % (HD // 2)).astype(F32) * 2.0 / HD))
    angles = jnp.arange(length).astype(F32)[:, None] * frequency[None, :]
    sign = jnp.where(lanes % HD < HD // 2, -1.0, 1.0)
    return jnp.cos(angles), jnp.sin(angles) * sign[None, :]


def slot_of(place, mine):
    turn = place ^ mine
    return ((turn & 1) << 1) | (turn >> 1)


def spot_of(place, mine, rows):
    return pl.ds(pl.multiple_of(slot_of(place, mine) * rows, rows), rows)


def partner(values):
    lane = lax.broadcasted_iota(jnp.int32, values.shape, 1)
    ahead = pltpu.roll(values, 2 * HD - HD // 2, 1)
    behind = pltpu.roll(values, HD // 2, 1)
    return jnp.where(lane % HD < HD // 2, ahead, behind)


def fetch(blocks, whole, done):
    copies, start = [], 0
    for i, block in enumerate(blocks):
        spot = whole.at[pl.ds(start, block.shape[0])]
        copies.append(pltpu.make_async_copy(block, spot, done.at[i]))
        copies[-1].start()
        start += block.shape[0]
    for copy in copies:
        copy.wait()


def forward_kernel(heads, rows, count, m_ref, *refs):
    blocks, refs = refs[:count], refs[count:]
    weight_ref, cos_ref, sin_ref, mixed_ref, qt_ref, kv_ref, lse_ref, normed_ref, done = refs
    fetch(blocks, normed_ref, done)
    mine = m_ref[0]
    width = heads * HD
    blocks = GROUP
    is_key = lax.broadcasted_iota(jnp.int32, (rows, 2 * HD), 1) < HD
    for p in range(blocks):
        span = slice(p * rows, (p + 1) * rows)
        qkv = dot(normed_ref[spot_of(p, mine, rows), :], weight_ref[...])
        cosine, sine = cos_ref[span, :], sin_ref[span, :]
        turned = []
        for start in range(0, width, 2 * HD):
            part = qkv[:, start : start + 2 * HD]
            turned.append(part * cosine + partner(part) * sine)
        query = jnp.concatenate(turned, axis=1) * HD ** (-0.5)
        qt_ref[0, :, span] = query.T.astype(BF16)
        part = qkv[:, width : width + 2 * HD]
        kv_ref[0, span, :] = jnp.where(
            is_key, part * cosine + partner(part) * sine, part
        ).astype(BF16)
    kv = kv_ref[0]
    vt = kv.astype(F32).T.astype(BF16)[HD:, :]
    keys = kv[:, :HD]
    ok = lax.broadcasted_iota(jnp.int32, (rows, rows), 0) <= lax.broadcasted_iota(
        jnp.int32, (rows, rows), 1
    )
    for p in range(blocks):
        span = slice(p * rows, (p + 1) * rows)
        outs, tops = [], []
        for h in range(heads):
            query = qt_ref[0, h * HD : (h + 1) * HD, span]
            last = jnp.where(ok, dot(keys[span], query), NEG)
            top = jnp.max(last, axis=0, keepdims=True)
            if p:
                first = dot(keys[: p * rows], query)
                top = jnp.maximum(top, jnp.max(first, axis=0, keepdims=True))
            weight = jnp.exp(last - top)
            total = jnp.sum(weight, axis=0, keepdims=True)
            if p:
                first = jnp.exp(first - top)
                total = total + jnp.sum(first, axis=0, keepdims=True)
            share = 1.0 / total
            out = dot(vt[:, span], (weight * share).astype(BF16))
            if p:
                out = out + dot(vt[:, : p * rows], (first * share).astype(BF16))
            outs.append(out)
            tops.append(top + jnp.log(total))
        mixed_ref[0, slot_of(p, mine)] = jnp.concatenate(outs, axis=0).T.astype(BF16)
        tops += [tops[0]] * (8 - heads)
        lse_ref[0, :, span] = jnp.concatenate(tops, axis=0)


def backward_kernel(heads, rows, count, m_ref, *refs):
    blocks, refs = refs[:count], refs[count:]
    qt_ref, kv_ref, lse_ref, out_ref, cos_ref, sin_ref, *refs = refs
    dq_ref, kept_ref, sent_ref, dk_sum, dv_sum, branch_ref, done = refs
    fetch(blocks, branch_ref, done)
    mine = m_ref[0]
    width = heads * HD
    blocks = GROUP
    kv = kv_ref[0]
    kt = kv.astype(F32).T.astype(BF16)[:HD, :]
    keys = kv[:, :HD]
    values = pltpu.roll(kv.astype(F32), HD, 1).astype(BF16)[:, :HD]
    ok = lax.broadcasted_iota(jnp.int32, (rows, rows), 0) <= lax.broadcasted_iota(
        jnp.int32, (rows, rows), 1
    )
    for p in reversed(range(blocks)):
        span = slice(p * rows, (p + 1) * rows)
        reach = (p + 1) * rows
        grad = thin(times_transposed(out_ref[...], branch_ref[spot_of(p, mine, rows), :]))
        dqs = []
        for h in range(heads):
            query = qt_ref[0, h * HD : (h + 1) * HD, span]
            above = grad[h * HD : (h + 1) * HD, :]
            lse = lse_ref[0, h : h + 1, span]
            scores = dot(keys[:reach], query)
            if p:
                scores = jnp.concatenate(
                    [scores[: p * rows], jnp.where(ok, scores[p * rows :], NEG)], axis=0
                )
            else:
                scores = jnp.where(ok, scores, NEG)
            probs = jnp.exp(scores - lse)
            probs_grad = dot(values[:reach], above)
            delta = jnp.sum(probs * probs_grad, axis=0, keepdims=True)
            score_low = (probs * (probs_grad - delta)).astype(BF16)
            dk = times_transposed(score_low, query)
            dv = times_transposed(probs.astype(BF16), above)
            if p == blocks - 1 and h == 0:
                dk_sum[...] = dk
                dv_sum[...] = dv
            else:
                dk_sum[:reach, :] += dk
                dv_sum[:reach, :] += dv
            dqs.append(dot(kt[:, :reach], score_low))
        dq = jnp.concatenate(dqs, axis=0).T * HD ** (-0.5)
        cosine, sine = cos_ref[span, :], sin_ref[span, :]
        turned = []
        for start in range(0, width, 2 * HD):
            part = dq[:, start : start + 2 * HD]
            turned.append(part * cosine - partner(part) * sine)
        dq_ref[0, slot_of(p, mine)] = jnp.concatenate(turned, axis=1).astype(BF16)
    is_key = lax.broadcasted_iota(jnp.int32, (rows, 2 * HD), 1) < HD
    for p in range(blocks):
        span = slice(p * rows, (p + 1) * rows)
        part = jnp.concatenate([dk_sum[span, :], dv_sum[span, :]], axis=1)
        cosine, sine = cos_ref[span, :], sin_ref[span, :]
        part = jnp.where(is_key, part * cosine - partner(part) * sine, part)
        turned = pltpu.roll(part, HD, 1)
        even = (mine & 1) == 0
        kept_ref[0, slot_of(p, mine)] = jnp.where(even, part, turned)[:, :HD]
        sent_ref[0, slot_of(p, mine ^ 1)] = jnp.where(even, turned, part)[:, :HD]


def same_spec(shape):
    zeros = (0,) * len(shape)
    return pl.BlockSpec(shape, lambda i, m: zeros)


def attention_call(kernel, mine, blocks, others, shapes, scratch, name):
    length = sum(block.shape[0] for block in blocks)
    return pl.pallas_call(
        kernel,
        grid_spec=pltpu.PrefetchScalarGridSpec(
            num_scalar_prefetch=1,
            grid=(1,),
            in_specs=[ANY] * len(blocks) + [same_spec(v.shape) for v in others],
            out_specs=[same_spec(shape) for shape, _ in shapes],
            scratch_shapes=scratch
            + [
                pltpu.VMEM((length, blocks[0].shape[1]), BF16),
                pltpu.SemaphoreType.DMA((len(blocks),)),
            ],
        ),
        out_shape=[jax.ShapeDtypeStruct(shape, dtype) for shape, dtype in shapes],
        compiler_params=pltpu.CompilerParams(vmem_limit_bytes=48 * 2**20),
        cost_estimate=WORK,
        name=name,
    )(mine, *blocks, *others)


def attend(blocks, weight, tables, mine, heads):
    length = tables[0].shape[0]
    rows, width = length // GROUP, heads * HD
    shapes = (
        ((1, GROUP, rows, width), BF16),
        ((1, width, length), BF16),
        ((1, length, 2 * HD), BF16),
        ((1, 8, length), F32),
    )
    kernel = functools.partial(forward_kernel, heads, rows, len(blocks))
    return attention_call(kernel, mine, blocks, (weight, *tables), shapes, [], "attend")


def attend_back(kept, blocks, out_weight, tables, mine, heads):
    length = tables[0].shape[0]
    rows, width = length // GROUP, heads * HD
    half = ((1, GROUP, rows, HD), F32)
    shapes = (((1, GROUP, rows, width), BF16), half, half)
    scratch = [pltpu.VMEM((length, HD), F32), pltpu.VMEM((length, HD), F32)]
    kernel = functools.partial(backward_kernel, heads, rows, len(blocks))
    others = (*kept, out_weight, *tables)
    return attention_call(kernel, mine, blocks, others, shapes, scratch, "attend_back")


class Clock:
    def __init__(self):
        self.past = ()

    def __call__(self, value):
        return after(value, *self.past) if self.past else value

    def tick(self, *values):
        self.past = values


def per_device(
    tokens, attn_gain, w_query, w_key, w_value, w_out, mlp_gain, w_gate, w_up, w_down, cotangent
):
    n = lax.axis_size("dev")
    planes = n // RANKS
    me = lax.axis_index("dev")
    plane, rank = me // RANKS, lax.rem(me, RANKS)
    core = lax.rem(me, 2)
    mine = lax.rem(me, GROUP).astype(jnp.int32).reshape(1)
    count, model = tokens.shape
    local = w_query.shape[0]
    heads = w_query.shape[1] // HD // RANKS
    kv_heads = w_key.shape[1] // HD
    width = heads * HD
    units = w_gate.shape[1] // n
    own_units = units * planes
    seqs = RANKS // GROUP
    share = RANKS // kv_heads

    to_rank = [(i, (i % planes) * RANKS + i // planes) for i in range(n)]
    from_rank = [(j, i) for i, j in to_rank]
    attn_cols = width + 2 * HD
    clock = Clock()

    def finish(ring, *tail):
        while len(ring) < planes:
            ring = ring + [onward(ring[-1])]
        return ring

    (attn_parts,) = on_rows(
        attn_parts_kernel,
        (w_query, w_key, w_value),
        (((RANKS, local, attn_cols), BF16),),
        "attn_parts",
    )
    attn_own = exchange(attn_parts).reshape(RANKS * local, attn_cols)
    gains = after(jnp.stack([attn_gain, mlp_gain]), attn_parts)
    gain_ring = [gains]
    for step in range(1, planes):
        route = [(i, (i + RANKS * step) % n) for i in range(n)]
        gain_ring.append(lax.ppermute(gains, "dev", route))
    gains = place_gains(gain_ring, plane)
    for bit in (1, 2, 4):
        gains = join_gains(gains, swap(gains, bit), bit, me)
    gain_rows = gains.reshape(planes, 2, -1).transpose(1, 0, 2)
    gain_one, gain_two = jnp.split(gain_rows.reshape(2, model).astype(F32), 2)
    out_ring = [lax.ppermute(after(w_out, attn_parts), "dev", to_rank)]
    (mlp_parts,) = on_rows(
        functools.partial(mlp_parts_kernel, units),
        (w_gate, w_up),
        (((RANKS, local, 2 * own_units), BF16),),
        "mlp_parts",
    )
    tables = rope_tables(GROUP * count)
    clock.tick(gain_one, gain_two, mlp_parts, *tables)
    attn_own = clock(attn_own)
    clock.tick(attn_own, out_ring[0])
    two, four = gather_pair(clock(tokens))
    attn_ring = [attn_own, onward(clock(attn_own))]
    clock.tick(attn_ring[1])
    attn_ring.append(onward(clock(attn_ring[1])))
    out_ring.append(onward(clock(out_ring[0])))
    clock.tick(two, four, attn_ring[2], out_ring[1])
    six = gather_last(clock(two), clock(four))
    attn_ring.append(onward(clock(attn_ring[2])))
    near_even = normed(gain_one, clock(tokens), two)
    near_odd = swap(near_even, 1)
    out_ring.append(onward(clock(out_ring[1])))
    clock.tick(near_odd, attn_ring[3], out_ring[2], *six)
    mlp_own = exchange(clock(mlp_parts)).reshape(RANKS * local, 2 * own_units)
    attn_weight = place_rows(finish([clock(block) for block in attn_ring]), plane)
    far_even = normed(gain_one, clock(four), *six)
    far_odd = swap(far_even, 1)
    clock.tick(attn_weight, far_even)
    out_ring.append(onward(clock(out_ring[2])))
    down_ring = [w_down, onward(clock(w_down))]
    above_two, above_four = gather_pair(clock(cotangent))

    near_one_even, near_one_odd, far_one_even, far_one_odd = near_even, near_odd, far_even, far_odd
    near_mixed, *near_kept = attend((clock(near_even), near_odd), attn_weight, tables, mine, heads)
    clock.tick(near_mixed, far_odd, out_ring[3], mlp_own, down_ring[1])
    down_ring.append(onward(clock(down_ring[1])))
    mlp_weight = planes_gather(clock(mlp_own))
    far_mixed, *far_kept = attend((clock(far_even), far_odd), attn_weight, tables, mine, heads)
    far_mixed, near_mixed = far_mixed.reshape(-1, width), near_mixed.reshape(-1, width)
    clock.tick(far_mixed, above_two, above_four, down_ring[2])
    down_ring.append(onward(clock(down_ring[2])))
    above_six = gather_last(clock(above_two), clock(above_four))
    out_weight = place_rows(finish([clock(block) for block in out_ring]), plane)
    odd = parts_of(True, False, clock(near_mixed), far_mixed, out_weight)
    peer = swap(odd, 1)
    even = parts_of(False, False, after(near_mixed, odd), far_mixed, out_weight)
    clock.tick(even, peer, *above_six)
    parts = (clock(even), peer)
    clock.tick(*send_rows(parts))
    arrived = cross(*(clock(part) for part in clock.past))
    even_above = join(clock(cotangent), above_two, above_four, *above_six)
    odd_above = swap(even_above, 1)
    clock.tick(*arrived, odd_above)
    arrived = [clock(part) for part in arrived]
    last = cross(*pass_rows(parts, arrived))
    clock.tick(*last)
    last = [clock(part) for part in last]
    middle, own_two, scale_two = on_rows(
        middle_kernel,
        (tokens, gain_two, *parts, *arrived, *last),
        (((count, model), F32), ((count, model), BF16), ((count, 1), F32)),
        "middle",
    )

    clock.tick(own_two)
    two, four = gather_pair(clock(own_two))
    clock.tick(two, four)
    six = gather_last(clock(two), clock(four))
    clock.tick(*six, down_ring[3])
    even_two = join(clock(own_two), two, four, *six)
    odd_two = swap(even_two, 1)
    down_weight = place_rows(finish([clock(part) for part in down_ring]), plane)
    clock.tick(even_two, mlp_weight)
    mlp_weight = join(clock(mlp_weight))

    def feed(normed):
        both = dot(normed, mlp_weight)
        gate, up_proj = both[:, :own_units], both[:, own_units:]
        return gate, up_proj, thin(gate * jax.nn.sigmoid(gate) * up_proj)

    even_gate, even_up, even_hidden = feed(clock(even_two))
    clock.tick(even_hidden, odd_two)
    odd_gate, odd_up, odd_hidden = feed(clock(odd_two))
    clock.tick(odd_hidden)
    out_odd = thin(dot(clock(odd_hidden), down_weight))
    out_peer = swap(out_odd, 1)
    out_even = thin(dot(after(even_hidden, out_odd), down_weight))
    clock.tick(out_even, out_peer)
    out_parts = (clock(out_even), out_peer)
    clock.tick(*send_rows(out_parts))
    out_arrived = cross(*(clock(part) for part in clock.past))
    down_sum = contract_rows(clock(even_hidden), even_above) + contract_rows(odd_hidden, odd_above)
    down_sum = thin(down_sum)
    clock.tick(down_sum)
    down_grad = planes_reduce(clock(down_sum)).astype(F32)

    def feed_back(above, gate, up_proj):
        sigmoid_gate = jax.nn.sigmoid(gate)
        hidden_grad = times_transposed(above, down_weight)
        gate_low = hidden_grad * up_proj * sigmoid_gate * (1.0 + gate * (1.0 - sigmoid_gate))
        return jnp.concatenate([thin(gate_low), thin(hidden_grad * gate * sigmoid_gate)], axis=1)

    odd_low = feed_back(clock(odd_above), odd_gate, odd_up)
    odd_part = thin(times_transposed(odd_low, mlp_weight))
    peer = swap(odd_part, 1)
    clock.tick(odd_part, *out_arrived)
    out_arrived = [clock(part) for part in out_arrived]
    out_last = cross(*pass_rows(out_parts, out_arrived))
    even_low = feed_back(clock(even_above), even_gate, even_up)
    parts = (thin(times_transposed(even_low, mlp_weight)), peer)
    clock.tick(*send_rows(parts), *out_last)
    arrived = cross(*clock.past[:2])
    (output,) = on_rows(
        output_kernel,
        (middle, *out_parts, *out_arrived, *[clock(part) for part in out_last]),
        (((count, model), BF16),),
        "output",
    )
    mlp_sum = contract_rows(clock(even_two), even_low)
    mlp_sum = thin(mlp_sum + contract_rows(clock(odd_two), odd_low))
    clock.tick(*arrived, mlp_sum, output, down_grad)
    mlp_total = planes_reduce(clock(mlp_sum))
    arrived = [clock(part) for part in arrived]
    last = cross(*pass_rows(parts, arrived))
    clock.tick(*last)
    last = [clock(part) for part in last]
    middle_grad, branch = on_rows(
        middle_back_kernel,
        (cotangent, gain_two, middle, scale_two, *parts, *arrived, *last),
        (((count, model), F32), ((count, model), BF16)),
        "middle_back",
    )

    clock.tick(branch)
    one = swap(clock(branch), 1)
    two, four = gather_pair(clock(branch))
    near_one, far_one = join(clock(near_one_even), near_one_odd), join(clock(far_one_even), far_one_odd)
    back_weight = jnp.concatenate(
        [
            clock(attn_weight)[:, :width],
            jnp.where(core == 0, attn_weight[:, width : width + HD], attn_weight[:, width + HD :]),
        ],
        axis=1,
    )
    clock.tick(one, two, four, near_one, far_one, back_weight)
    six = gather_last(clock(two), clock(four))
    three = swap(clock(two), 1)
    clock.tick(three)

    def attention_back(kept, *blocks):
        query_low, own, other = attend_back(kept, blocks, out_weight, tables, mine, heads)
        return query_low.reshape(-1, width), own.reshape(-1, HD), swap(other.reshape(-1, HD), 1)

    near_blocks = (clock(branch), two, one, three)
    near_query, near_own, near_other = attention_back(near_kept, *near_blocks)
    clock.tick(near_query, *six)
    far_even = join(clock(four), *six)
    far_odd = swap(far_even, 1)
    near_branch = join(*near_blocks)
    clock.tick(far_odd, near_branch, near_other)
    far_query, far_own, far_other = attention_back(far_kept, clock(far_even), far_odd)
    near_all = jnp.concatenate([near_query, thin(near_own + near_other)], axis=1)
    clock.tick(far_query, far_other, near_all)
    far_all = jnp.concatenate([clock(far_query), thin(far_own + far_other)], axis=1)
    far_branch = join(clock(far_even), far_odd)
    odd = parts_of(True, True, near_all, far_all, back_weight)
    peer = swap(odd, 1)
    even = parts_of(False, True, after(near_all, odd), far_all, back_weight)
    out_sum = contract_rows(after(near_mixed, even), near_branch) + contract_rows(far_mixed, far_branch)
    out_hop = onward(ring_start(out_sum, plane, planes))
    attn_sum = contract_rows(after(near_one, out_sum), near_all) + contract_rows(after(far_one, out_sum), far_all)
    clock.tick(even, peer, attn_sum)
    parts = (clock(even), peer)
    clock.tick(*send_rows(parts), mlp_total)
    arrived = cross(*clock.past[:2])
    mlp_back = exchange(clock(mlp_total).reshape(RANKS, local, 2 * own_units))
    attn_hop = onward(clock(ring_start(attn_sum, plane, planes)))
    clock.tick(attn_hop, out_hop)
    attn_hop = onward(ring_add(attn_sum, 1, clock(attn_hop), plane, planes))
    out_hop = onward(ring_add(out_sum, 1, clock(out_hop), plane, planes))
    clock.tick(*arrived)
    arrived = [clock(part) for part in arrived]
    last = cross(*pass_rows(parts, arrived))
    clock.tick(attn_hop, out_hop)
    attn_hop = onward(ring_add(attn_sum, 2, clock(attn_hop), plane, planes))
    out_hop = onward(ring_add(out_sum, 2, clock(out_hop), plane, planes))
    clock.tick(*last, mlp_back)
    mlp_back = clock(mlp_back)
    last = [clock(part) for part in last]
    (input_grad,) = on_rows(
        input_back_kernel,
        (middle_grad, gain_one, tokens, *parts, *arrived, *last),
        (((count, model), BF16),),
        "input_back",
    )
    clock.tick(attn_hop, out_hop, input_grad)
    for step in range(3, planes - 1):
        attn_hop = onward(ring_add(attn_sum, step, attn_hop, plane, planes))
        out_hop = onward(ring_add(out_sum, step, out_hop, plane, planes))
    out_total = ring_add(out_sum, planes - 1, clock(out_hop), plane, planes)
    attn_total = ring_add(attn_sum, planes - 1, clock(attn_hop), plane, planes)
    attn_back = exchange(thin(attn_total).reshape(RANKS, local, width + HD))
    out_grad = lax.ppermute(out_total, "dev", from_rank)

    gate_grad, up_grad, mlp_gain_sum = on_rows(
        functools.partial(mlp_back_kernel, units),
        (mlp_back, w_gate, w_up),
        ((w_gate.shape, F32), (w_up.shape, F32), ((local, 1), F32)),
        "mlp_back",
    )
    query_grad, key_grad, value_grad, attn_gain_sum = on_rows(
        attn_back_kernel,
        (attn_back, w_query, w_key, w_value),
        ((w_query.shape, F32), (w_key.shape, F32), (w_value.shape, F32), ((local, 1), F32)),
        "attn_back",
    )
    return (
        output,
        input_grad,
        attn_gain_sum[:, 0] / attn_gain,
        query_grad,
        key_grad,
        value_grad,
        out_grad,
        mlp_gain_sum[:, 0] / mlp_gain,
        gate_grad,
        up_grad,
        down_grad,
    )


def solution(mesh):
    row, vec = P("dev", None), P("dev")
    return jax.shard_map(
        per_device,
        mesh=mesh,
        in_specs=(row, vec, row, row, row, row, vec, row, row, row, row),
        out_specs=(row, row, vec, row, row, row, row, vec, row, row, row),
        check_vma=False,
    )
```

```python
import functools

import jax
import jax.numpy as jnp
from jax import lax
from jax.experimental import pallas as pl
from jax.experimental.pallas import tpu as pltpu
from jax.sharding import PartitionSpec as P

HD = 64
RANKS = 8
GROUP = 4
EPS = 1e-05
THETA = 10000.0
NEG = -1e30
F32 = jnp.float32
ANY = pl.BlockSpec(memory_space=pl.ANY)
SCALAR = pl.BlockSpec(memory_space=pltpu.SMEM)
WORK = pl.CostEstimate(flops=1, bytes_accessed=1, transcendentals=0)
BF16 = jnp.bfloat16


def swap(block, bit):
    n = lax.axis_size("dev")
    return lax.ppermute(block, "dev", [(i, i ^ bit) for i in range(n)])


def onward(block):
    n = lax.axis_size("dev")
    return lax.ppermute(block, "dev", [(i, (i + RANKS) % n) for i in range(n)])


def plane_groups():
    n = lax.axis_size("dev")
    return [[p * RANKS + r for r in range(RANKS)] for p in range(n // RANKS)]


def exchange(blocks):
    return lax.all_to_all(
        blocks, "dev", split_axis=0, concat_axis=0, tiled=True, axis_index_groups=plane_groups()
    )


def column_groups():
    n = lax.axis_size("dev")
    return [[p * RANKS + r for p in range(n // RANKS)] for r in range(RANKS)]


def planes_gather(block):
    return lax.all_gather(block, "dev", axis=0, tiled=True, axis_index_groups=column_groups())


def planes_reduce(terms):
    return lax.psum_scatter(
        terms, "dev", scatter_dimension=0, tiled=True, axis_index_groups=column_groups()
    )


def after(value, *earlier):
    return lax.optimization_barrier((value,) + earlier)[0]


def wide(value):
    return value.astype(F32)


def thin(value):
    return value.astype(BF16)


def copy_kernel(count, spots, first_ref, *refs):
    blocks, whole, done = refs[:count], refs[count], refs[count + 1]
    copies = []
    for i, block in enumerate(blocks):
        spot = whole.at[pl.ds(spots(i, first_ref[0]), block.shape[0])]
        copies.append(pltpu.make_async_copy(block, spot, done.at[i]))
        copies[-1].start()
    for copy in copies:
        copy.wait()


def copied(blocks, spots, first, name):
    rows = sum(block.shape[0] for block in blocks)
    return pl.pallas_call(
        functools.partial(copy_kernel, len(blocks), spots),
        in_specs=[SCALAR] + [ANY] * len(blocks),
        out_shape=jax.ShapeDtypeStruct((rows, blocks[0].shape[1]), blocks[0].dtype),
        compiler_params=pltpu.CompilerParams(vmem_limit_bytes=40 * 2**20),
        scratch_shapes=[pltpu.SemaphoreType.DMA((len(blocks),))],
        cost_estimate=WORK,
        name=name,
    )(first, *blocks)


def join(*blocks):
    starts = [0]
    for block in blocks:
        starts.append(starts[-1] + block.shape[0])
    return copied(blocks, lambda i, _: starts[i], jnp.zeros(1, jnp.int32), "join")


def gather_pair(block):
    return swap(block, 2), swap(block, 4)


def gather_last(two, four):
    half = two.shape[0] // 2
    return swap(two[:half], 4), swap(four[half:], 2)


def on_rows(function, ins, outs, name):
    return pl.pallas_call(
        function,
        out_shape=[jax.ShapeDtypeStruct(shape, dtype) for shape, dtype in outs],
        compiler_params=pltpu.CompilerParams(vmem_limit_bytes=40 * 2**20),
        cost_estimate=WORK,
        name=name,
    )(*ins)


def sliced_kernel(function, spans, whole, count, *refs):
    distant, refs = refs[:whole], refs[whole:]
    others, refs = refs[:count], refs[count:]
    outs, held, done = refs[: -len(spans) - 1], refs[-len(spans) - 1 : -1], refs[-1]
    copies = []
    for i, (which, start, rows) in enumerate(spans):
        source = distant[which].at[pl.ds(start, rows)]
        copies.append(pltpu.make_async_copy(source, held[i], done.at[i]))
        copies[-1].start()
    for copy in copies:
        copy.wait()
    function(*others, *held, *outs)


def on_spans(function, spans, others, outs, name, mebibytes=40):
    arrays = []
    for array, _, _ in spans:
        if not any(array is known for known in arrays):
            arrays.append(array)
    which = lambda array: next(i for i, known in enumerate(arrays) if array is known)
    places = tuple((which(array), start, rows) for array, start, rows in spans)
    vmem = pl.BlockSpec(memory_space=pltpu.VMEM)
    return pl.pallas_call(
        functools.partial(sliced_kernel, function, places, len(arrays), len(others)),
        in_specs=[ANY] * len(arrays) + [vmem] * len(others),
        out_shape=[jax.ShapeDtypeStruct(shape, dtype) for shape, dtype in outs],
        scratch_shapes=[pltpu.VMEM((rows, array.shape[1]), array.dtype) for array, _, rows in spans]
        + [pltpu.SemaphoreType.DMA((len(spans),))],
        compiler_params=pltpu.CompilerParams(vmem_limit_bytes=mebibytes * 2**20),
        cost_estimate=WORK,
        name=name,
    )(*arrays, *others)


def both(parts, start, rows):
    return [(part, start, rows) for part in parts]


def send_kernel(two_even, two_peer, four_even, four_peer, six_even, six_peer, to_two, to_four):
    half = two_even.shape[0]
    to_two[:half] = thin(wide(two_even[...]) + wide(two_peer[...]))
    to_four[:half] = thin(wide(four_even[...]) + wide(four_peer[...]))
    to_two[half:] = thin(wide(six_even[:half]) + wide(six_peer[:half]))
    to_four[half:] = thin(wide(six_even[half:]) + wide(six_peer[half:]))


def pass_kernel(four_even, four_peer, two_even, two_peer, from_two, from_four, to_two, to_four):
    to_four[...] = thin(wide(four_even[...]) + wide(four_peer[...]) + wide(from_two[...]))
    to_two[...] = thin(wide(two_even[...]) + wide(two_peer[...]) + wide(from_four[...]))


def send_rows(parts):
    rows, cols = parts[0].shape
    block, half = rows // 4, rows // 8
    spans = both(parts, block, half) + both(parts, 2 * block + half, half)
    spans += both(parts, 3 * block, block)
    shape = ((block, cols), BF16)
    return on_spans(send_kernel, spans, (), (shape, shape), "send_rows")


def pass_rows(parts, arrived, mebibytes=40):
    rows, cols = parts[0].shape
    block, half = rows // 4, rows // 8
    spans = both(parts, 2 * block, half) + both(parts, block + half, half)
    spans += [(part, half, half) for part in arrived]
    shape = ((half, cols), BF16)
    return on_spans(pass_kernel, spans, (), (shape, shape), "pass_rows", mebibytes)


def cross(to_two, to_four):
    return swap(to_two, 2), swap(to_four, 4)


def own_spans(parts, arrived, last):
    rows = parts[0].shape[0] // 4
    half = rows // 2
    first = [(part, 0, half) for part in arrived]
    return both(parts, 0, rows) + first + [(part, 0, half) for part in last]


def block_sum(even, peer, from_two, from_four, last_two, last_four):
    rows = last_two.shape[0]
    top, low = slice(0, rows), slice(rows, 2 * rows)
    upper = wide(even[top]) + wide(peer[top]) + wide(from_two[...]) + wide(last_four[...])
    lower = wide(even[low]) + wide(peer[low]) + wide(from_four[...]) + wide(last_two[...])
    return jnp.concatenate([upper, lower], axis=0)


def parts_kernel(odd, transposed, near, far, weight, out):
    half = near.shape[0] // 2
    span = slice(half, 2 * half) if odd else slice(0, half)
    multiply = times_transposed if transposed else dot
    out[:half] = thin(multiply(near[span], weight[...]))
    out[half:] = thin(multiply(far[span], weight[...]))


def parts_of(odd, transposed, near, far, weight):
    cols = weight.shape[0 if transposed else 1]
    return on_rows(
        functools.partial(parts_kernel, odd, transposed),
        (near, far, weight),
        (((near.shape[0], cols), BF16),),
        "odd_parts" if odd else "even_parts",
    )[0]


def mean_of(values):
    return jnp.mean(values, axis=1, keepdims=True)


def norm_kernel(gain, *refs):
    out, start = refs[-1], 0
    for block in refs[:-1]:
        values = wide(block[...])
        span = slice(start, start + block.shape[0])
        out[span] = thin(values * rms_scale(values) * gain[...])
        start += block.shape[0]


def normed(gain, *blocks):
    rows = sum(block.shape[0] for block in blocks)
    shape = (rows, blocks[0].shape[1])
    return on_rows(norm_kernel, (gain, *blocks), ((shape, BF16),), "norm")[0]


def middle_kernel(tokens, gain, *refs):
    sums, (middle_ref, normed_ref, scale_ref) = refs[:6], refs[6:]
    middle = wide(tokens[...]) + block_sum(*sums)
    scale = rms_scale(middle)
    middle_ref[...] = middle
    normed_ref[...] = thin(middle * scale * gain[...])
    scale_ref[...] = scale


def middle_back_kernel(above, gain, middle, scale, *refs):
    sums, (grad_ref, branch_ref) = refs[:6], refs[6:]
    scaled = block_sum(*sums) * gain[...]
    middle, scale = middle[...], scale[...]
    grad = wide(above[...]) + scale * scaled - middle * scale**3 * mean_of(scaled * middle)
    grad_ref[...] = grad
    branch_ref[...] = thin(grad)


def output_kernel(middle, *refs):
    refs[-1][...] = thin(middle[...] + block_sum(*refs[:6]))


def input_back_kernel(grad, gain, tokens, *refs):
    scaled = block_sum(*refs[:6]) * gain[...]
    source = wide(tokens[...])
    scale = rms_scale(source)
    whole = grad[...] + scale * scaled - source * scale**3 * mean_of(scaled * source)
    refs[-1][...] = thin(whole)


def attn_parts_kernel(query, key, value, parts):
    width = query.shape[1] // RANKS
    share = RANKS * HD // key.shape[1]
    for j in range(RANKS):
        head = slice(j // share * HD, (j // share + 1) * HD)
        parts[j, :, :width] = query[:, j * width : (j + 1) * width]
        parts[j, :, width:] = jnp.concatenate([key[:, head], value[:, head]], axis=1)


def mlp_parts_kernel(units, gate, up, parts):
    planes = gate.shape[1] // units // RANKS
    for j in range(RANKS):
        pieces = []
        for weight in (gate, up):
            for p in range(planes):
                start = (p * RANKS + j) * units
                pieces.append(weight[:, start : start + units])
        parts[j] = jnp.concatenate(pieces, axis=1)


def lane_sums(grad, weight):
    total = 0.0
    for start in range(0, grad.shape[1], 128):
        span = slice(start, start + 128)
        total = total + grad[:, span] * wide(weight[:, span])
    return jnp.sum(total, axis=1, keepdims=True)


def mlp_back_kernel(units, parts, gate, up, gate_grad, up_grad, gain_sum):
    planes = gate.shape[1] // units // RANKS
    own = planes * units
    for half, grad in enumerate((gate_grad, up_grad)):
        for p in range(planes):
            start = half * own + p * units
            pieces = [parts[j, :, start : start + units] for j in range(RANKS)]
            row = jnp.concatenate(pieces, axis=1)
            grad[:, p * RANKS * units : (p + 1) * RANKS * units] = wide(row)
    gain_sum[...] = lane_sums(gate_grad, gate) + lane_sums(up_grad, up)


def attn_back_kernel(parts, query, key, value, query_grad, key_grad, value_grad, gain_sum):
    width = query.shape[1] // RANKS
    share = RANKS * HD // key.shape[1]
    for j in range(RANKS):
        query_grad[:, j * width : (j + 1) * width] = wide(parts[j, :, :width])
    for first, grad in enumerate((key_grad, value_grad)):
        pieces = [parts[j, :, width:] for j in range(first, RANKS, share)]
        grad[...] = wide(jnp.concatenate(pieces, axis=1))
    gain_sum[...] = (
        lane_sums(query_grad, query) + lane_sums(key_grad, key) + lane_sums(value_grad, value)
    )


def place_rows(blocks, plane):
    planes, rows = len(blocks), blocks[0].shape[0]

    def spot(step, own):
        return lax.rem(own + planes - step, planes) * rows

    if rows % 16 == 0:
        aligned = lambda step, own: pl.multiple_of(spot(step, own), 16)
        return copied(blocks, aligned, plane.astype(jnp.int32).reshape(1), "place_rows")
    whole = jnp.zeros((planes * rows, blocks[0].shape[1]), blocks[0].dtype)
    for step, block in enumerate(blocks):
        whole = lax.dynamic_update_slice_in_dim(whole, block, spot(step, plane), 0)
    return whole


def place_gains(blocks, plane):
    planes, rows = len(blocks), blocks[0].shape[0]
    whole = jnp.zeros((planes * rows, blocks[0].shape[1]), blocks[0].dtype)
    for step, block in enumerate(blocks):
        place = lax.rem(plane + planes - step, planes)
        whole = lax.dynamic_update_slice_in_dim(whole, block, place * rows, 0)
    return whole


def join_gains(gains, other, bit, me):
    return jnp.where(
        me & bit,
        jnp.concatenate([other, gains], axis=1),
        jnp.concatenate([gains, other], axis=1),
    )


def ring_part(terms, step, plane, planes):
    rows = terms.shape[0] // planes
    place = lax.rem(plane + 2 * planes - 1 - step, planes)
    return lax.dynamic_slice_in_dim(terms, place * rows, rows, 0)


def ring_start(terms, plane, planes):
    return thin(ring_part(terms, 0, plane, planes))


def ring_add(terms, step, arrived, plane, planes):
    total = ring_part(terms, step, plane, planes) + wide(arrived)
    return thin(total) if step < planes - 1 else total


def dot(left, right):
    return jnp.dot(left, right, preferred_element_type=F32)


def contract_rows(left, right):
    return lax.dot_general(left, right, (((0,), (0,)), ((), ())), preferred_element_type=F32)


def times_transposed(left, right):
    return lax.dot_general(left, right, (((1,), (1,)), ((), ())), preferred_element_type=F32)


def rms_scale(values):
    return lax.rsqrt(jnp.mean(values * values, axis=1, keepdims=True) + EPS)


def rope_tables(length):
    lanes = jnp.arange(2 * HD)
    frequency = THETA ** (-((lanes % (HD // 2)).astype(F32) * 2.0 / HD))
    angles = jnp.arange(length).astype(F32)[:, None] * frequency[None, :]
    sign = jnp.where(lanes % HD < HD // 2, -1.0, 1.0)
    return jnp.cos(angles), jnp.sin(angles) * sign[None, :]


def slot_of(place, mine):
    turn = place ^ mine
    return ((turn & 1) << 1) | (turn >> 1)


def spot_of(place, mine, rows):
    return pl.ds(pl.multiple_of(slot_of(place, mine) * rows, rows), rows)


def partner(values):
    lane = lax.broadcasted_iota(jnp.int32, values.shape, 1)
    ahead = pltpu.roll(values, 2 * HD - HD // 2, 1)
    behind = pltpu.roll(values, HD // 2, 1)
    return jnp.where(lane % HD < HD // 2, ahead, behind)


def fetch(blocks, whole, done):
    copies, start = [], 0
    for i, block in enumerate(blocks):
        spot = whole.at[pl.ds(start, block.shape[0])]
        copies.append(pltpu.make_async_copy(block, spot, done.at[i]))
        copies[-1].start()
        start += block.shape[0]
    for copy in copies:
        copy.wait()


def heads_beside(stacked, heads):
    return jnp.concatenate([stacked[h * HD : (h + 1) * HD] for h in range(heads)], axis=1)


def heads_below(beside, heads):
    rows = beside.shape[1] // heads
    return jnp.concatenate([beside[:, h * rows : (h + 1) * rows] for h in range(heads)], axis=0)


def causal(rows, heads):
    key = lax.broadcasted_iota(jnp.int32, (rows, heads * rows), 0)
    query = lax.broadcasted_iota(jnp.int32, (rows, heads * rows), 1)
    return key <= query % rows


def forward_kernel(heads, rows, count, m_ref, *refs):
    blocks, refs = refs[:count], refs[count:]
    weight_ref, cos_ref, sin_ref, mixed_ref, qt_ref, kv_ref, lse_ref, normed_ref, done = refs
    fetch(blocks, normed_ref, done)
    mine = m_ref[0]
    width = heads * HD
    is_key = lax.broadcasted_iota(jnp.int32, (rows, 2 * HD), 1) < HD
    ok = causal(rows, heads)
    for p in range(GROUP):
        span = slice(p * rows, (p + 1) * rows)
        qkv = dot(normed_ref[spot_of(p, mine, rows), :], weight_ref[...])
        cosine, sine = cos_ref[span, :], sin_ref[span, :]
        turned = []
        for start in range(0, width, 2 * HD):
            part = qkv[:, start : start + 2 * HD]
            turned.append(part * cosine + partner(part) * sine)
        query = jnp.concatenate(turned, axis=1) * HD ** (-0.5)
        qt_ref[0, p] = heads_beside(query.T, heads).astype(BF16)
        part = qkv[:, width : width + 2 * HD]
        kv_ref[0, span, :] = jnp.where(
            is_key, part * cosine + partner(part) * sine, part
        ).astype(BF16)
    kv = kv_ref[0]
    vt = kv.astype(F32).T.astype(BF16)[HD:, :]
    keys = kv[:, :HD]
    for p in range(GROUP):
        span = slice(p * rows, (p + 1) * rows)
        query = qt_ref[0, p]
        last = jnp.where(ok, dot(keys[span], query), NEG)
        top = jnp.max(last, axis=0, keepdims=True)
        if p:
            first = dot(keys[: p * rows], query)
            top = jnp.maximum(top, jnp.max(first, axis=0, keepdims=True))
        last = jnp.exp(last - top)
        total = jnp.sum(last, axis=0, keepdims=True)
        if p:
            first = jnp.exp(first - top)
            total = total + jnp.sum(first, axis=0, keepdims=True)
        share = 1.0 / total
        out = dot(vt[:, span], (last * share).astype(BF16))
        if p:
            out = out + dot(vt[:, : p * rows], (first * share).astype(BF16))
        mixed_ref[0, slot_of(p, mine)] = heads_below(out, heads).T.astype(BF16)
        lse_ref[0, p] = top + jnp.log(total)


def backward_kernel(heads, rows, count, m_ref, *refs):
    blocks, refs = refs[:count], refs[count:]
    qt_ref, kv_ref, lse_ref, out_ref, cos_ref, sin_ref, *refs = refs
    dq_ref, kept_ref, sent_ref, dk_sum, dv_sum, branch_ref, done = refs
    fetch(blocks, branch_ref, done)
    mine = m_ref[0]
    width = heads * HD
    kv = kv_ref[0]
    kt = kv.astype(F32).T.astype(BF16)[:HD, :]
    keys = kv[:, :HD]
    values = pltpu.roll(kv.astype(F32), HD, 1).astype(BF16)[:, :HD]
    ok = causal(rows, heads)
    for p in reversed(range(GROUP)):
        span = slice(p * rows, (p + 1) * rows)
        reach = (p + 1) * rows
        grad = thin(times_transposed(out_ref[...], branch_ref[spot_of(p, mine, rows), :]))
        above = heads_beside(grad, heads)
        query = qt_ref[0, p]
        scores = dot(keys[:reach], query)
        last = jnp.where(ok, scores[p * rows :], NEG)
        scores = jnp.concatenate([scores[: p * rows], last], axis=0) if p else last
        probs = jnp.exp(scores - lse_ref[0, p])
        probs_grad = dot(values[:reach], above)
        delta = jnp.sum(probs * probs_grad, axis=0, keepdims=True)
        score_low = (probs * (probs_grad - delta)).astype(BF16)
        dk = times_transposed(score_low, query)
        dv = times_transposed(probs.astype(BF16), above)
        if p == GROUP - 1:
            dk_sum[...] = dk
            dv_sum[...] = dv
        else:
            dk_sum[:reach, :] += dk
            dv_sum[:reach, :] += dv
        dq = heads_below(dot(kt[:, :reach], score_low), heads).T * HD ** (-0.5)
        cosine, sine = cos_ref[span, :], sin_ref[span, :]
        turned = []
        for start in range(0, width, 2 * HD):
            part = dq[:, start : start + 2 * HD]
            turned.append(part * cosine - partner(part) * sine)
        dq_ref[0, slot_of(p, mine)] = jnp.concatenate(turned, axis=1).astype(BF16)
    is_key = lax.broadcasted_iota(jnp.int32, (rows, 2 * HD), 1) < HD
    for p in range(GROUP):
        span = slice(p * rows, (p + 1) * rows)
        part = jnp.concatenate([dk_sum[span, :], dv_sum[span, :]], axis=1)
        cosine, sine = cos_ref[span, :], sin_ref[span, :]
        part = jnp.where(is_key, part * cosine - partner(part) * sine, part)
        turned = pltpu.roll(part, HD, 1)
        even = (mine & 1) == 0
        kept_ref[0, slot_of(p, mine)] = jnp.where(even, part, turned)[:, :HD]
        sent_ref[0, slot_of(p, mine ^ 1)] = jnp.where(even, turned, part)[:, :HD]


def same_spec(shape):
    zeros = (0,) * len(shape)
    return pl.BlockSpec(shape, lambda i, m: zeros)


def attention_call(kernel, mine, blocks, others, shapes, scratch, name):
    length = sum(block.shape[0] for block in blocks)
    return pl.pallas_call(
        kernel,
        grid_spec=pltpu.PrefetchScalarGridSpec(
            num_scalar_prefetch=1,
            grid=(1,),
            in_specs=[ANY] * len(blocks) + [same_spec(v.shape) for v in others],
            out_specs=[same_spec(shape) for shape, _ in shapes],
            scratch_shapes=scratch
            + [
                pltpu.VMEM((length, blocks[0].shape[1]), BF16),
                pltpu.SemaphoreType.DMA((len(blocks),)),
            ],
        ),
        out_shape=[jax.ShapeDtypeStruct(shape, dtype) for shape, dtype in shapes],
        compiler_params=pltpu.CompilerParams(vmem_limit_bytes=48 * 2**20),
        cost_estimate=WORK,
        name=name,
    )(mine, *blocks, *others)


def attend(blocks, weight, tables, mine, heads):
    length = tables[0].shape[0]
    rows, width = length // GROUP, heads * HD
    shapes = (
        ((1, GROUP, rows, width), BF16),
        ((1, GROUP, HD, heads * rows), BF16),
        ((1, length, 2 * HD), BF16),
        ((1, GROUP, 1, heads * rows), F32),
    )
    kernel = functools.partial(forward_kernel, heads, rows, len(blocks))
    return attention_call(kernel, mine, blocks, (weight, *tables), shapes, [], "attend")


def attend_back(kept, blocks, out_weight, tables, mine, heads):
    length = tables[0].shape[0]
    rows, width = length // GROUP, heads * HD
    half = ((1, GROUP, rows, HD), F32)
    shapes = (((1, GROUP, rows, width), BF16), half, half)
    scratch = [pltpu.VMEM((length, HD), F32), pltpu.VMEM((length, HD), F32)]
    kernel = functools.partial(backward_kernel, heads, rows, len(blocks))
    others = (*kept, out_weight, *tables)
    return attention_call(kernel, mine, blocks, others, shapes, scratch, "attend_back")


class Clock:
    def __init__(self):
        self.past = ()

    def __call__(self, value):
        return after(value, *self.past) if self.past else value

    def tick(self, *values):
        self.past = values


def per_device(
    tokens, attn_gain, w_query, w_key, w_value, w_out, mlp_gain, w_gate, w_up, w_down, cotangent
):
    n = lax.axis_size("dev")
    planes = n // RANKS
    me = lax.axis_index("dev")
    plane, rank = me // RANKS, lax.rem(me, RANKS)
    core = lax.rem(me, 2)
    mine = lax.rem(me, GROUP).astype(jnp.int32).reshape(1)
    count, model = tokens.shape
    local = w_query.shape[0]
    heads = w_query.shape[1] // HD // RANKS
    kv_heads = w_key.shape[1] // HD
    width = heads * HD
    units = w_gate.shape[1] // n
    own_units = units * planes
    seqs = RANKS // GROUP
    share = RANKS // kv_heads

    to_rank = [(i, (i % planes) * RANKS + i // planes) for i in range(n)]
    from_rank = [(j, i) for i, j in to_rank]
    attn_cols = width + 2 * HD
    clock = Clock()

    def finish(ring, *tail):
        while len(ring) < planes:
            ring = ring + [onward(ring[-1])]
        return ring

    (attn_parts,) = on_rows(
        attn_parts_kernel,
        (w_query, w_key, w_value),
        (((RANKS, local, attn_cols), BF16),),
        "attn_parts",
    )
    attn_own = exchange(attn_parts).reshape(RANKS * local, attn_cols)
    gains = after(jnp.stack([attn_gain, mlp_gain]), attn_parts)
    gain_ring = [gains]
    for step in range(1, planes):
        route = [(i, (i + RANKS * step) % n) for i in range(n)]
        gain_ring.append(lax.ppermute(gains, "dev", route))
    gains = place_gains(gain_ring, plane)
    for bit in (1, 2, 4):
        gains = join_gains(gains, swap(gains, bit), bit, me)
    gain_rows = gains.reshape(planes, 2, -1).transpose(1, 0, 2)
    gain_one, gain_two = jnp.split(gain_rows.reshape(2, model).astype(F32), 2)
    out_ring = [lax.ppermute(after(w_out, attn_parts), "dev", to_rank)]
    (mlp_parts,) = on_rows(
        functools.partial(mlp_parts_kernel, units),
        (w_gate, w_up),
        (((RANKS, local, 2 * own_units), BF16),),
        "mlp_parts",
    )
    tables = rope_tables(GROUP * count)
    clock.tick(gain_one, gain_two, mlp_parts, *tables)
    attn_own = clock(attn_own)
    clock.tick(attn_own, out_ring[0])
    two, four = gather_pair(clock(tokens))
    attn_ring = [attn_own, onward(clock(attn_own))]
    clock.tick(attn_ring[1])
    attn_ring.append(onward(clock(attn_ring[1])))
    out_ring.append(onward(clock(out_ring[0])))
    clock.tick(two, four, attn_ring[2], out_ring[1])
    six = gather_last(clock(two), clock(four))
    attn_ring.append(onward(clock(attn_ring[2])))
    near_even = normed(gain_one, clock(tokens), two)
    near_odd = swap(near_even, 1)
    out_ring.append(onward(clock(out_ring[1])))
    clock.tick(near_odd, attn_ring[3], out_ring[2], *six)
    mlp_own = exchange(clock(mlp_parts)).reshape(RANKS * local, 2 * own_units)
    attn_weight = place_rows(finish([clock(block) for block in attn_ring]), plane)
    far_even = normed(gain_one, clock(four), *six)
    far_odd = swap(far_even, 1)
    clock.tick(attn_weight, far_even)
    out_ring.append(onward(clock(out_ring[2])))
    down_ring = [w_down, onward(clock(w_down))]

    near_one_even, near_one_odd, far_one_even, far_one_odd = near_even, near_odd, far_even, far_odd
    near_mixed, *near_kept = attend((clock(near_even), near_odd), attn_weight, tables, mine, heads)
    clock.tick(near_mixed, far_odd, mlp_own, down_ring[1])
    above_two, above_four = gather_pair(clock(cotangent))
    down_ring.append(onward(clock(down_ring[1])))
    mlp_weight = planes_gather(clock(mlp_own))
    far_mixed, *far_kept = attend((clock(far_even), far_odd), attn_weight, tables, mine, heads)
    far_mixed, near_mixed = far_mixed.reshape(-1, width), near_mixed.reshape(-1, width)
    clock.tick(far_mixed, out_ring[3])
    out_weight = place_rows(finish([clock(block) for block in out_ring]), plane)
    odd = parts_of(True, False, clock(near_mixed), far_mixed, out_weight)
    peer = swap(odd, 1)
    even = parts_of(False, False, after(near_mixed, odd), far_mixed, out_weight)
    clock.tick(even, peer)
    parts = (clock(even), peer)
    clock.tick(*send_rows(parts))
    arrived = cross(*(clock(part) for part in clock.past[:2]))
    clock.tick(*arrived, above_two, above_four)
    arrived = [clock(part) for part in arrived]
    last = cross(*pass_rows(parts, arrived))
    clock.tick(*last, down_ring[2])
    last = [clock(part) for part in last]
    middle, own_two, scale_two = on_spans(
        middle_kernel,
        own_spans(parts, arrived, last),
        (tokens, gain_two),
        (((count, model), F32), ((count, model), BF16), ((count, 1), F32)),
        "middle",
    )

    clock.tick(own_two)
    two, four = gather_pair(clock(own_two))
    clock.tick(two, four)
    six = gather_last(clock(two), clock(four))
    clock.tick(*six)
    even_two = join(clock(own_two), two, four, *six)
    odd_two = swap(even_two, 1)
    clock.tick(even_two)
    above_six = gather_last(clock(above_two), clock(above_four))
    clock.tick(mlp_weight, down_ring[2])
    down_ring.append(onward(clock(down_ring[2])))
    mlp_weight = join(clock(mlp_weight))

    def feed(normed):
        both = dot(normed, mlp_weight)
        gate, up_proj = both[:, :own_units], both[:, own_units:]
        return gate, up_proj, thin(gate * jax.nn.sigmoid(gate) * up_proj)

    even_gate, even_up, even_hidden = feed(clock(even_two))
    clock.tick(even_hidden, odd_two)
    even_above = join(clock(cotangent), above_two, above_four, *(clock(part) for part in above_six))
    odd_above = swap(even_above, 1)
    odd_gate, odd_up, odd_hidden = feed(clock(odd_two))
    clock.tick(odd_hidden, down_ring[3])
    down_weight = place_rows(finish([clock(part) for part in down_ring]), plane)
    out_odd = thin(dot(odd_hidden, down_weight))
    out_peer = swap(out_odd, 1)
    out_even = thin(dot(after(even_hidden, out_odd), down_weight))
    clock.tick(out_even, out_peer, odd_above)
    out_parts = (clock(out_even), out_peer)
    clock.tick(*send_rows(out_parts))
    out_arrived = cross(*(clock(part) for part in clock.past))
    down_sum = contract_rows(clock(even_hidden), even_above) + contract_rows(odd_hidden, odd_above)
    down_sum = thin(down_sum)
    clock.tick(down_sum)
    down_total = planes_reduce(clock(down_sum))

    def feed_back(above, gate, up_proj):
        sigmoid_gate = jax.nn.sigmoid(gate)
        hidden_grad = times_transposed(above, down_weight)
        gate_low = hidden_grad * up_proj * sigmoid_gate * (1.0 + gate * (1.0 - sigmoid_gate))
        return jnp.concatenate([thin(gate_low), thin(hidden_grad * gate * sigmoid_gate)], axis=1)

    odd_low = feed_back(clock(odd_above), odd_gate, odd_up)
    odd_part = thin(times_transposed(odd_low, mlp_weight))
    peer = swap(odd_part, 1)
    clock.tick(odd_part)
    even_low = feed_back(clock(even_above), even_gate, even_up)
    parts = (thin(times_transposed(even_low, mlp_weight)), peer)
    clock.tick(*send_rows(parts), *out_arrived)
    out_arrived = [clock(part) for part in out_arrived]
    arrived = cross(*clock.past[:2])
    mlp_sum = contract_rows(clock(even_two), even_low)
    clock.tick(*arrived, mlp_sum)
    arrived = [clock(part) for part in arrived]
    last = cross(*pass_rows(parts, arrived))
    mlp_sum = thin(mlp_sum + contract_rows(clock(odd_two), odd_low))
    clock.tick(*last, mlp_sum, down_total)
    mlp_total = planes_reduce(clock(mlp_sum))
    last = [clock(part) for part in last]
    middle_grad, branch = on_spans(
        middle_back_kernel,
        own_spans(parts, arrived, last),
        (cotangent, gain_two, middle, scale_two),
        (((count, model), F32), ((count, model), BF16)),
        "middle_back",
        60,
    )

    clock.tick(branch)
    one = swap(clock(branch), 1)
    two, four = gather_pair(clock(branch))
    near_one, far_one = join(clock(near_one_even), near_one_odd), join(clock(far_one_even), far_one_odd)
    back_weight = jnp.concatenate(
        [
            clock(attn_weight)[:, :width],
            jnp.where(core == 0, attn_weight[:, width : width + HD], attn_weight[:, width + HD :]),
        ],
        axis=1,
    )
    clock.tick(one, two, four, near_one, far_one, back_weight)
    six = gather_last(clock(two), clock(four))
    three = swap(clock(two), 1)
    clock.tick(three)

    def attention_back(kept, *blocks):
        query_low, own, other = attend_back(kept, blocks, out_weight, tables, mine, heads)
        return query_low.reshape(-1, width), own.reshape(-1, HD), swap(other.reshape(-1, HD), 1)

    near_blocks = (clock(branch), two, one, three)
    near_query, near_own, near_other = attention_back(near_kept, *near_blocks)
    clock.tick(near_query, *six)
    far_even = join(clock(four), *six)
    far_odd = swap(far_even, 1)
    near_branch = join(*near_blocks)
    clock.tick(far_odd, near_branch, near_other)
    far_branch = join(clock(far_even), far_odd)
    out_sum = contract_rows(clock(near_mixed), near_branch) + contract_rows(clock(far_mixed), far_branch)
    out_sum = thin(out_sum)
    clock.tick(out_sum, far_branch)
    far_query, far_own, far_other = attention_back(far_kept, clock(far_even), far_odd)
    near_all = jnp.concatenate([near_query, thin(near_own + near_other)], axis=1)
    clock.tick(far_query, far_other, near_all)
    far_all = jnp.concatenate([clock(far_query), thin(far_own + far_other)], axis=1)
    odd = parts_of(True, True, near_all, far_all, back_weight)
    peer = swap(odd, 1)
    even = parts_of(False, True, after(near_all, odd), far_all, back_weight)
    out_last = cross(*pass_rows(out_parts, [after(part, even) for part in out_arrived], 60))
    attn_sum = contract_rows(after(near_one, even), near_all) + contract_rows(after(far_one, even), far_all)
    clock.tick(even, peer, attn_sum)
    parts = (clock(even), peer)
    clock.tick(*send_rows(parts), mlp_total, *out_last)
    arrived = cross(*clock.past[:2])
    (output,) = on_spans(
        output_kernel,
        own_spans(out_parts, out_arrived, [clock(part) for part in out_last]),
        (middle,),
        (((count, model), BF16),),
        "output",
        60,
    )
    out_total = planes_reduce(clock(out_sum))
    mlp_back = exchange(clock(mlp_total).reshape(RANKS, local, 2 * own_units))
    attn_hop = onward(clock(ring_start(attn_sum, plane, planes)))
    clock.tick(attn_hop)
    attn_hop = onward(ring_add(attn_sum, 1, clock(attn_hop), plane, planes))
    clock.tick(*arrived, output)
    arrived = [clock(part) for part in arrived]
    last = cross(*pass_rows(parts, arrived, 60))
    clock.tick(attn_hop)
    attn_hop = onward(ring_add(attn_sum, 2, clock(attn_hop), plane, planes))
    clock.tick(*last, mlp_back, out_total)
    out_grad = lax.ppermute(clock(out_total), "dev", from_rank).astype(F32)
    mlp_back = clock(mlp_back)
    last = [clock(part) for part in last]
    (input_grad,) = on_spans(
        input_back_kernel,
        own_spans(parts, arrived, last),
        (middle_grad, gain_one, tokens),
        (((count, model), BF16),),
        "input_back",
        60,
    )
    clock.tick(attn_hop, input_grad)
    down_grad = clock(down_total).astype(F32)
    for step in range(3, planes - 1):
        attn_hop = onward(ring_add(attn_sum, step, attn_hop, plane, planes))
    attn_total = ring_add(attn_sum, planes - 1, clock(attn_hop), plane, planes)
    attn_back = exchange(thin(attn_total).reshape(RANKS, local, width + HD))

    gate_grad, up_grad, mlp_gain_sum = on_rows(
        functools.partial(mlp_back_kernel, units),
        (mlp_back, w_gate, w_up),
        ((w_gate.shape, F32), (w_up.shape, F32), ((local, 1), F32)),
        "mlp_back",
    )
    query_grad, key_grad, value_grad, attn_gain_sum = on_rows(
        attn_back_kernel,
        (attn_back, w_query, w_key, w_value),
        ((w_query.shape, F32), (w_key.shape, F32), (w_value.shape, F32), ((local, 1), F32)),
        "attn_back",
    )
    return (
        output,
        input_grad,
        attn_gain_sum[:, 0] / attn_gain,
        query_grad,
        key_grad,
        value_grad,
        out_grad,
        mlp_gain_sum[:, 0] / mlp_gain,
        gate_grad,
        up_grad,
        down_grad,
    )


def solution(mesh):
    row, vec = P("dev", None), P("dev")
    return jax.shard_map(
        per_device,
        mesh=mesh,
        in_specs=(row, vec, row, row, row, row, vec, row, row, row, row),
        out_specs=(row, row, vec, row, row, row, row, vec, row, row, row),
        check_vma=False,
    )
```

```python
import functools

import jax
import jax.numpy as jnp
from jax import lax
from jax.experimental import pallas as pl
from jax.experimental.pallas import tpu as pltpu
from jax.sharding import PartitionSpec as P

HD = 64
RANKS = 8
GROUP = 4
EPS = 1e-05
THETA = 10000.0
NEG = -1e30
F32 = jnp.float32
ANY = pl.BlockSpec(memory_space=pl.ANY)
SCALAR = pl.BlockSpec(memory_space=pltpu.SMEM)
WORK = pl.CostEstimate(flops=2 * 10**9, bytes_accessed=1, transcendentals=0)
BF16 = jnp.bfloat16


def swap(block, bit):
    n = lax.axis_size("dev")
    return lax.ppermute(block, "dev", [(i, i ^ bit) for i in range(n)])


def onward(block):
    n = lax.axis_size("dev")
    return lax.ppermute(block, "dev", [(i, (i + RANKS) % n) for i in range(n)])


def plane_groups():
    n = lax.axis_size("dev")
    return [[p * RANKS + r for r in range(RANKS)] for p in range(n // RANKS)]


def exchange(blocks):
    return lax.all_to_all(
        blocks, "dev", split_axis=0, concat_axis=0, tiled=True, axis_index_groups=plane_groups()
    )


def column_groups():
    n = lax.axis_size("dev")
    return [[p * RANKS + r for p in range(n // RANKS)] for r in range(RANKS)]


def planes_gather(block):
    return lax.all_gather(block, "dev", axis=0, tiled=True, axis_index_groups=column_groups())


def planes_reduce(terms):
    return lax.psum_scatter(
        terms, "dev", scatter_dimension=0, tiled=True, axis_index_groups=column_groups()
    )


def after(value, *earlier):
    return lax.optimization_barrier((value,) + earlier)[0]


def wide(value):
    return value.astype(F32)


def thin(value):
    return value.astype(BF16)


def copy_kernel(count, spots, first_ref, *refs):
    blocks, whole, done = refs[:count], refs[count], refs[count + 1]
    copies = []
    for i, block in enumerate(blocks):
        spot = whole.at[pl.ds(spots(i, first_ref[0]), block.shape[0])]
        copies.append(pltpu.make_async_copy(block, spot, done.at[i]))
        copies[-1].start()
    for copy in copies:
        copy.wait()


def copied(blocks, spots, first, name):
    rows = sum(block.shape[0] for block in blocks)
    return pl.pallas_call(
        functools.partial(copy_kernel, len(blocks), spots),
        in_specs=[SCALAR] + [ANY] * len(blocks),
        out_shape=jax.ShapeDtypeStruct((rows, blocks[0].shape[1]), blocks[0].dtype),
        compiler_params=pltpu.CompilerParams(vmem_limit_bytes=40 * 2**20),
        scratch_shapes=[pltpu.SemaphoreType.DMA((len(blocks),))],
        cost_estimate=WORK,
        name=name,
    )(first, *blocks)


def join(*blocks):
    starts = [0]
    for block in blocks:
        starts.append(starts[-1] + block.shape[0])
    return copied(blocks, lambda i, _: starts[i], jnp.zeros(1, jnp.int32), "join")


def gather_pair(block):
    return swap(block, 2), swap(block, 4)


def gather_last(two, four):
    half = two.shape[0] // 2
    return swap(two[:half], 4), swap(four[half:], 2)


def on_rows(function, ins, outs, name):
    return pl.pallas_call(
        function,
        out_shape=[jax.ShapeDtypeStruct(shape, dtype) for shape, dtype in outs],
        compiler_params=pltpu.CompilerParams(vmem_limit_bytes=40 * 2**20),
        cost_estimate=WORK,
        name=name,
    )(*ins)


def sliced_kernel(function, spans, whole, count, *refs):
    distant, refs = refs[:whole], refs[whole:]
    others, refs = refs[:count], refs[count:]
    outs, held, done = refs[: -len(spans) - 1], refs[-len(spans) - 1 : -1], refs[-1]
    copies = []
    for i, (which, start, rows) in enumerate(spans):
        source = distant[which].at[pl.ds(start, rows)]
        copies.append(pltpu.make_async_copy(source, held[i], done.at[i]))
        copies[-1].start()
    for copy in copies:
        copy.wait()
    function(*others, *held, *outs)


def on_spans(function, spans, others, outs, name, mebibytes=40):
    arrays = []
    for array, _, _ in spans:
        if not any(array is known for known in arrays):
            arrays.append(array)
    which = lambda array: next(i for i, known in enumerate(arrays) if array is known)
    places = tuple((which(array), start, rows) for array, start, rows in spans)
    vmem = pl.BlockSpec(memory_space=pltpu.VMEM)
    return pl.pallas_call(
        functools.partial(sliced_kernel, function, places, len(arrays), len(others)),
        in_specs=[ANY] * len(arrays) + [vmem] * len(others),
        out_shape=[jax.ShapeDtypeStruct(shape, dtype) for shape, dtype in outs],
        scratch_shapes=[pltpu.VMEM((rows, array.shape[1]), array.dtype) for array, _, rows in spans]
        + [pltpu.SemaphoreType.DMA((len(spans),))],
        compiler_params=pltpu.CompilerParams(vmem_limit_bytes=mebibytes * 2**20),
        cost_estimate=WORK,
        name=name,
    )(*arrays, *others)


def both(parts, start, rows):
    return [(part, start, rows) for part in parts]


def send_kernel(two_even, two_peer, four_even, four_peer, six_even, six_peer, to_two, to_four):
    half = two_even.shape[0]
    to_two[:half] = thin(wide(two_even[...]) + wide(two_peer[...]))
    to_four[:half] = thin(wide(four_even[...]) + wide(four_peer[...]))
    to_two[half:] = thin(wide(six_even[:half]) + wide(six_peer[:half]))
    to_four[half:] = thin(wide(six_even[half:]) + wide(six_peer[half:]))


def pass_kernel(four_even, four_peer, two_even, two_peer, from_two, from_four, to_two, to_four):
    to_four[...] = thin(wide(four_even[...]) + wide(four_peer[...]) + wide(from_two[...]))
    to_two[...] = thin(wide(two_even[...]) + wide(two_peer[...]) + wide(from_four[...]))


def send_rows(parts):
    rows, cols = parts[0].shape
    block, half = rows // 4, rows // 8
    spans = both(parts, block, half) + both(parts, 2 * block + half, half)
    spans += both(parts, 3 * block, block)
    shape = ((block, cols), BF16)
    return on_spans(send_kernel, spans, (), (shape, shape), "send_rows")


def pass_rows(parts, arrived, mebibytes=40):
    rows, cols = parts[0].shape
    block, half = rows // 4, rows // 8
    spans = both(parts, 2 * block, half) + both(parts, block + half, half)
    spans += [(part, half, half) for part in arrived]
    shape = ((half, cols), BF16)
    return on_spans(pass_kernel, spans, (), (shape, shape), "pass_rows", mebibytes)


def cross(to_two, to_four):
    return swap(to_two, 2), swap(to_four, 4)


def own_spans(parts, arrived, last):
    rows = parts[0].shape[0] // 4
    half = rows // 2
    first = [(part, 0, half) for part in arrived]
    return both(parts, 0, rows) + first + [(part, 0, half) for part in last]


def block_sum(even, peer, from_two, from_four, last_two, last_four):
    rows = last_two.shape[0]
    top, low = slice(0, rows), slice(rows, 2 * rows)
    upper = wide(even[top]) + wide(peer[top]) + wide(from_two[...]) + wide(last_four[...])
    lower = wide(even[low]) + wide(peer[low]) + wide(from_four[...]) + wide(last_two[...])
    return jnp.concatenate([upper, lower], axis=0)


def parts_kernel(odd, transposed, near, far, weight, out):
    half = near.shape[0] // 2
    span = slice(half, 2 * half) if odd else slice(0, half)
    multiply = times_transposed if transposed else dot
    out[:half] = thin(multiply(near[span], weight[...]))
    out[half:] = thin(multiply(far[span], weight[...]))


def parts_of(odd, transposed, near, far, weight):
    cols = weight.shape[0 if transposed else 1]
    return on_rows(
        functools.partial(parts_kernel, odd, transposed),
        (near, far, weight),
        (((near.shape[0], cols), BF16),),
        "odd_parts" if odd else "even_parts",
    )[0]


def mean_of(values):
    return jnp.mean(values, axis=1, keepdims=True)


def norm_kernel(gain, *refs):
    out, start = refs[-1], 0
    for block in refs[:-1]:
        values = wide(block[...])
        span = slice(start, start + block.shape[0])
        out[span] = thin(values * rms_scale(values) * gain[...])
        start += block.shape[0]


def normed(gain, *blocks):
    rows = sum(block.shape[0] for block in blocks)
    shape = (rows, blocks[0].shape[1])
    return on_rows(norm_kernel, (gain, *blocks), ((shape, BF16),), "norm")[0]


def middle_kernel(tokens, gain, *refs):
    sums, (middle_ref, normed_ref, scale_ref) = refs[:6], refs[6:]
    middle = wide(tokens[...]) + block_sum(*sums)
    scale = rms_scale(middle)
    middle_ref[...] = middle
    normed_ref[...] = thin(middle * scale * gain[...])
    scale_ref[...] = scale


def middle_back_kernel(above, gain, middle, scale, *refs):
    sums, (grad_ref, branch_ref) = refs[:6], refs[6:]
    scaled = block_sum(*sums) * gain[...]
    middle, scale = middle[...], scale[...]
    grad = wide(above[...]) + scale * scaled - middle * scale**3 * mean_of(scaled * middle)
    grad_ref[...] = grad
    branch_ref[...] = thin(grad)


def output_kernel(middle, *refs):
    refs[-1][...] = thin(middle[...] + block_sum(*refs[:6]))


def input_back_kernel(grad, gain, tokens, *refs):
    scaled = block_sum(*refs[:6]) * gain[...]
    source = wide(tokens[...])
    scale = rms_scale(source)
    whole = grad[...] + scale * scaled - source * scale**3 * mean_of(scaled * source)
    refs[-1][...] = thin(whole)


def attn_parts_kernel(query, key, value, parts):
    width = query.shape[1] // RANKS
    share = RANKS * HD // key.shape[1]
    for j in range(RANKS):
        head = slice(j // share * HD, (j // share + 1) * HD)
        parts[j, :, :width] = query[:, j * width : (j + 1) * width]
        parts[j, :, width:] = jnp.concatenate([key[:, head], value[:, head]], axis=1)


def mlp_parts_kernel(units, gate, up, parts):
    planes = gate.shape[1] // units // RANKS
    for j in range(RANKS):
        pieces = []
        for weight in (gate, up):
            for p in range(planes):
                start = (p * RANKS + j) * units
                pieces.append(weight[:, start : start + units])
        parts[j] = jnp.concatenate(pieces, axis=1)


def lane_sums(grad, weight):
    total = 0.0
    for start in range(0, grad.shape[1], 128):
        span = slice(start, start + 128)
        total = total + grad[:, span] * wide(weight[:, span])
    return jnp.sum(total, axis=1, keepdims=True)


def mlp_back_kernel(units, parts, gate, up, gate_grad, up_grad, gain_sum):
    planes = gate.shape[1] // units // RANKS
    own = planes * units
    for half, grad in enumerate((gate_grad, up_grad)):
        for p in range(planes):
            start = half * own + p * units
            pieces = [parts[j, :, start : start + units] for j in range(RANKS)]
            row = jnp.concatenate(pieces, axis=1)
            grad[:, p * RANKS * units : (p + 1) * RANKS * units] = wide(row)
    gain_sum[...] = lane_sums(gate_grad, gate) + lane_sums(up_grad, up)


def attn_back_kernel(parts, query, key, value, query_grad, key_grad, value_grad, gain_sum):
    width = query.shape[1] // RANKS
    share = RANKS * HD // key.shape[1]
    for j in range(RANKS):
        query_grad[:, j * width : (j + 1) * width] = wide(parts[j, :, :width])
    for first, grad in enumerate((key_grad, value_grad)):
        pieces = [parts[j, :, width:] for j in range(first, RANKS, share)]
        grad[...] = wide(jnp.concatenate(pieces, axis=1))
    gain_sum[...] = (
        lane_sums(query_grad, query) + lane_sums(key_grad, key) + lane_sums(value_grad, value)
    )


def place_rows(blocks, plane):
    planes, rows = len(blocks), blocks[0].shape[0]

    def spot(step, own):
        return lax.rem(own + planes - step, planes) * rows

    if rows % 16 == 0:
        aligned = lambda step, own: pl.multiple_of(spot(step, own), 16)
        return copied(blocks, aligned, plane.astype(jnp.int32).reshape(1), "place_rows")
    whole = jnp.zeros((planes * rows, blocks[0].shape[1]), blocks[0].dtype)
    for step, block in enumerate(blocks):
        whole = lax.dynamic_update_slice_in_dim(whole, block, spot(step, plane), 0)
    return whole


def place_gains(blocks, plane):
    planes, rows = len(blocks), blocks[0].shape[0]
    whole = jnp.zeros((planes * rows, blocks[0].shape[1]), blocks[0].dtype)
    for step, block in enumerate(blocks):
        place = lax.rem(plane + planes - step, planes)
        whole = lax.dynamic_update_slice_in_dim(whole, block, place * rows, 0)
    return whole


def join_gains(gains, other, bit, me):
    return jnp.where(
        me & bit,
        jnp.concatenate([other, gains], axis=1),
        jnp.concatenate([gains, other], axis=1),
    )


def ring_part(terms, step, plane, planes):
    rows = terms.shape[0] // planes
    place = lax.rem(plane + 2 * planes - 1 - step, planes)
    return lax.dynamic_slice_in_dim(terms, place * rows, rows, 0)


def ring_start(terms, plane, planes):
    return thin(ring_part(terms, 0, plane, planes))


def ring_add(terms, step, arrived, plane, planes):
    total = ring_part(terms, step, plane, planes) + wide(arrived)
    return thin(total) if step < planes - 1 else total


def dot(left, right):
    return jnp.dot(left, right, preferred_element_type=F32)


def contract_rows(left, right):
    return lax.dot_general(left, right, (((0,), (0,)), ((), ())), preferred_element_type=F32)


def times_transposed(left, right):
    return lax.dot_general(left, right, (((1,), (1,)), ((), ())), preferred_element_type=F32)


def rms_scale(values):
    return lax.rsqrt(jnp.mean(values * values, axis=1, keepdims=True) + EPS)


def rope_tables(length):
    lanes = jnp.arange(2 * HD)
    frequency = THETA ** (-((lanes % (HD // 2)).astype(F32) * 2.0 / HD))
    angles = jnp.arange(length).astype(F32)[:, None] * frequency[None, :]
    sign = jnp.where(lanes % HD < HD // 2, -1.0, 1.0)
    return jnp.cos(angles), jnp.sin(angles) * sign[None, :]


def slot_of(place, mine):
    turn = place ^ mine
    return ((turn & 1) << 1) | (turn >> 1)


def spot_of(place, mine, rows):
    return pl.ds(pl.multiple_of(slot_of(place, mine) * rows, rows), rows)


def partner(values):
    lane = lax.broadcasted_iota(jnp.int32, values.shape, 1)
    ahead = pltpu.roll(values, 2 * HD - HD // 2, 1)
    behind = pltpu.roll(values, HD // 2, 1)
    return jnp.where(lane % HD < HD // 2, ahead, behind)


def fetch(blocks, whole, done):
    copies, start = [], 0
    for i, block in enumerate(blocks):
        spot = whole.at[pl.ds(start, block.shape[0])]
        copies.append(pltpu.make_async_copy(block, spot, done.at[i]))
        copies[-1].start()
        start += block.shape[0]
    for copy in copies:
        copy.wait()


def heads_beside(stacked, heads):
    return jnp.concatenate([stacked[h * HD : (h + 1) * HD] for h in range(heads)], axis=1)


def heads_below(beside, heads):
    rows = beside.shape[1] // heads
    return jnp.concatenate([beside[:, h * rows : (h + 1) * rows] for h in range(heads)], axis=0)


def causal(rows, heads):
    key = lax.broadcasted_iota(jnp.int32, (rows, heads * rows), 0)
    query = lax.broadcasted_iota(jnp.int32, (rows, heads * rows), 1)
    return key <= query % rows


def forward_kernel(heads, rows, count, m_ref, *refs):
    blocks, refs = refs[:count], refs[count:]
    weight_ref, cos_ref, sin_ref, mixed_ref, qt_ref, kv_ref, lse_ref, normed_ref, done = refs
    fetch(blocks, normed_ref, done)
    mine = m_ref[0]
    width = heads * HD
    is_key = lax.broadcasted_iota(jnp.int32, (rows, 2 * HD), 1) < HD
    ok = causal(rows, heads)
    for p in range(GROUP):
        span = slice(p * rows, (p + 1) * rows)
        qkv = dot(normed_ref[spot_of(p, mine, rows), :], weight_ref[...])
        cosine, sine = cos_ref[span, :], sin_ref[span, :]
        turned = []
        for start in range(0, width, 2 * HD):
            part = qkv[:, start : start + 2 * HD]
            turned.append(part * cosine + partner(part) * sine)
        query = jnp.concatenate(turned, axis=1) * HD ** (-0.5)
        qt_ref[0, p] = heads_beside(query.T, heads).astype(BF16)
        part = qkv[:, width : width + 2 * HD]
        kv_ref[0, span, :] = jnp.where(
            is_key, part * cosine + partner(part) * sine, part
        ).astype(BF16)
    kv = kv_ref[0]
    vt = kv.astype(F32).T.astype(BF16)[HD:, :]
    keys = kv[:, :HD]
    for p in range(GROUP):
        span = slice(p * rows, (p + 1) * rows)
        query = qt_ref[0, p]
        last = jnp.where(ok, dot(keys[span], query), NEG)
        top = jnp.max(last, axis=0, keepdims=True)
        if p:
            first = dot(keys[: p * rows], query)
            top = jnp.maximum(top, jnp.max(first, axis=0, keepdims=True))
        last = jnp.exp(last - top)
        total = jnp.sum(last, axis=0, keepdims=True)
        if p:
            first = jnp.exp(first - top)
            total = total + jnp.sum(first, axis=0, keepdims=True)
        share = 1.0 / total
        out = dot(vt[:, span], (last * share).astype(BF16))
        if p:
            out = out + dot(vt[:, : p * rows], (first * share).astype(BF16))
        mixed_ref[0, slot_of(p, mine)] = heads_below(out, heads).T.astype(BF16)
        lse_ref[0, p] = top + jnp.log(total)


def backward_kernel(heads, rows, count, m_ref, *refs):
    blocks, refs = refs[:count], refs[count:]
    qt_ref, kv_ref, lse_ref, out_ref, cos_ref, sin_ref, *refs = refs
    dq_ref, kept_ref, sent_ref, dk_sum, dv_sum, branch_ref, done = refs
    fetch(blocks, branch_ref, done)
    mine = m_ref[0]
    width = heads * HD
    kv = kv_ref[0]
    kt = kv.astype(F32).T.astype(BF16)[:HD, :]
    keys = kv[:, :HD]
    values = pltpu.roll(kv.astype(F32), HD, 1).astype(BF16)[:, :HD]
    ok = causal(rows, heads)
    for p in reversed(range(GROUP)):
        span = slice(p * rows, (p + 1) * rows)
        reach = (p + 1) * rows
        grad = thin(times_transposed(out_ref[...], branch_ref[spot_of(p, mine, rows), :]))
        above = heads_beside(grad, heads)
        query = qt_ref[0, p]
        scores = dot(keys[:reach], query)
        last = jnp.where(ok, scores[p * rows :], NEG)
        scores = jnp.concatenate([scores[: p * rows], last], axis=0) if p else last
        probs = jnp.exp(scores - lse_ref[0, p])
        probs_grad = dot(values[:reach], above)
        delta = jnp.sum(probs * probs_grad, axis=0, keepdims=True)
        score_low = (probs * (probs_grad - delta)).astype(BF16)
        dk = times_transposed(score_low, query)
        dv = times_transposed(probs.astype(BF16), above)
        if p == GROUP - 1:
            dk_sum[...] = dk
            dv_sum[...] = dv
        else:
            dk_sum[:reach, :] += dk
            dv_sum[:reach, :] += dv
        dq = heads_below(dot(kt[:, :reach], score_low), heads).T * HD ** (-0.5)
        cosine, sine = cos_ref[span, :], sin_ref[span, :]
        turned = []
        for start in range(0, width, 2 * HD):
            part = dq[:, start : start + 2 * HD]
            turned.append(part * cosine - partner(part) * sine)
        dq_ref[0, slot_of(p, mine)] = jnp.concatenate(turned, axis=1).astype(BF16)
    is_key = lax.broadcasted_iota(jnp.int32, (rows, 2 * HD), 1) < HD
    for p in range(GROUP):
        span = slice(p * rows, (p + 1) * rows)
        part = jnp.concatenate([dk_sum[span, :], dv_sum[span, :]], axis=1)
        cosine, sine = cos_ref[span, :], sin_ref[span, :]
        part = jnp.where(is_key, part * cosine - partner(part) * sine, part)
        turned = pltpu.roll(part, HD, 1)
        even = (mine & 1) == 0
        kept_ref[0, slot_of(p, mine)] = jnp.where(even, part, turned)[:, :HD]
        sent_ref[0, slot_of(p, mine ^ 1)] = jnp.where(even, turned, part)[:, :HD]


def same_spec(shape):
    zeros = (0,) * len(shape)
    return pl.BlockSpec(shape, lambda i, m: zeros)


def attention_call(kernel, mine, blocks, others, shapes, scratch, name):
    length = sum(block.shape[0] for block in blocks)
    return pl.pallas_call(
        kernel,
        grid_spec=pltpu.PrefetchScalarGridSpec(
            num_scalar_prefetch=1,
            grid=(1,),
            in_specs=[ANY] * len(blocks) + [same_spec(v.shape) for v in others],
            out_specs=[same_spec(shape) for shape, _ in shapes],
            scratch_shapes=scratch
            + [
                pltpu.VMEM((length, blocks[0].shape[1]), BF16),
                pltpu.SemaphoreType.DMA((len(blocks),)),
            ],
        ),
        out_shape=[jax.ShapeDtypeStruct(shape, dtype) for shape, dtype in shapes],
        compiler_params=pltpu.CompilerParams(vmem_limit_bytes=48 * 2**20),
        cost_estimate=WORK,
        name=name,
    )(mine, *blocks, *others)


def attend(blocks, weight, tables, mine, heads):
    length = tables[0].shape[0]
    rows, width = length // GROUP, heads * HD
    shapes = (
        ((1, GROUP, rows, width), BF16),
        ((1, GROUP, HD, heads * rows), BF16),
        ((1, length, 2 * HD), BF16),
        ((1, GROUP, 1, heads * rows), F32),
    )
    kernel = functools.partial(forward_kernel, heads, rows, len(blocks))
    return attention_call(kernel, mine, blocks, (weight, *tables), shapes, [], "attend")


def attend_back(kept, blocks, out_weight, tables, mine, heads):
    length = tables[0].shape[0]
    rows, width = length // GROUP, heads * HD
    half = ((1, GROUP, rows, HD), F32)
    shapes = (((1, GROUP, rows, width), BF16), half, half)
    scratch = [pltpu.VMEM((length, HD), F32), pltpu.VMEM((length, HD), F32)]
    kernel = functools.partial(backward_kernel, heads, rows, len(blocks))
    others = (*kept, out_weight, *tables)
    return attention_call(kernel, mine, blocks, others, shapes, scratch, "attend_back")


class Clock:
    def __init__(self):
        self.past = ()

    def __call__(self, value):
        return after(value, *self.past) if self.past else value

    def tick(self, *values):
        self.past = values


def per_device(
    tokens, attn_gain, w_query, w_key, w_value, w_out, mlp_gain, w_gate, w_up, w_down, cotangent
):
    n = lax.axis_size("dev")
    planes = n // RANKS
    me = lax.axis_index("dev")
    plane, rank = me // RANKS, lax.rem(me, RANKS)
    core = lax.rem(me, 2)
    mine = lax.rem(me, GROUP).astype(jnp.int32).reshape(1)
    count, model = tokens.shape
    local = w_query.shape[0]
    heads = w_query.shape[1] // HD // RANKS
    kv_heads = w_key.shape[1] // HD
    width = heads * HD
    units = w_gate.shape[1] // n
    own_units = units * planes
    seqs = RANKS // GROUP
    share = RANKS // kv_heads

    to_rank = [(i, (i % planes) * RANKS + i // planes) for i in range(n)]
    from_rank = [(j, i) for i, j in to_rank]
    attn_cols = width + 2 * HD
    clock = Clock()

    def finish(ring, *tail):
        while len(ring) < planes:
            ring = ring + [onward(ring[-1])]
        return ring

    (attn_parts,) = on_rows(
        attn_parts_kernel,
        (w_query, w_key, w_value),
        (((RANKS, local, attn_cols), BF16),),
        "attn_parts",
    )
    attn_own = exchange(attn_parts).reshape(RANKS * local, attn_cols)
    gains = after(jnp.stack([attn_gain, mlp_gain]), attn_parts)
    gain_ring = [gains]
    for step in range(1, planes):
        route = [(i, (i + RANKS * step) % n) for i in range(n)]
        gain_ring.append(lax.ppermute(gains, "dev", route))
    gains = place_gains(gain_ring, plane)
    for bit in (1, 2, 4):
        gains = join_gains(gains, swap(gains, bit), bit, me)
    gain_rows = gains.reshape(planes, 2, -1).transpose(1, 0, 2)
    gain_one, gain_two = jnp.split(gain_rows.reshape(2, model).astype(F32), 2)
    out_ring = [lax.ppermute(after(w_out, attn_parts), "dev", to_rank)]
    (mlp_parts,) = on_rows(
        functools.partial(mlp_parts_kernel, units),
        (w_gate, w_up),
        (((RANKS, local, 2 * own_units), BF16),),
        "mlp_parts",
    )
    tables = rope_tables(GROUP * count)
    clock.tick(gain_one, gain_two, mlp_parts, *tables)
    attn_own = clock(attn_own)
    clock.tick(attn_own, out_ring[0])
    two, four = gather_pair(clock(tokens))
    attn_ring = [attn_own, onward(clock(attn_own))]
    clock.tick(attn_ring[1])
    attn_ring.append(onward(clock(attn_ring[1])))
    out_ring.append(onward(clock(out_ring[0])))
    clock.tick(two, four, attn_ring[2], out_ring[1])
    six = gather_last(clock(two), clock(four))
    attn_ring.append(onward(clock(attn_ring[2])))
    near_even = normed(gain_one, clock(tokens), two)
    near_odd = swap(near_even, 1)
    out_ring.append(onward(clock(out_ring[1])))
    clock.tick(near_odd, attn_ring[3], out_ring[2], *six)
    mlp_own = exchange(clock(mlp_parts)).reshape(RANKS * local, 2 * own_units)
    attn_weight = place_rows(finish([clock(block) for block in attn_ring]), plane)
    far_even = normed(gain_one, clock(four), *six)
    far_odd = swap(far_even, 1)
    clock.tick(attn_weight, far_even)
    out_ring.append(onward(clock(out_ring[2])))
    down_ring = [w_down, onward(clock(w_down))]

    near_one_even, near_one_odd, far_one_even, far_one_odd = near_even, near_odd, far_even, far_odd
    near_mixed, *near_kept = attend((clock(near_even), near_odd), attn_weight, tables, mine, heads)
    clock.tick(near_mixed, far_odd, mlp_own, down_ring[1])
    above_two, above_four = gather_pair(clock(cotangent))
    down_ring.append(onward(clock(down_ring[1])))
    mlp_weight = planes_gather(clock(mlp_own))
    far_mixed, *far_kept = attend((clock(far_even), far_odd), attn_weight, tables, mine, heads)
    far_mixed, near_mixed = far_mixed.reshape(-1, width), near_mixed.reshape(-1, width)
    clock.tick(far_mixed, out_ring[3])
    out_weight = place_rows(finish([clock(block) for block in out_ring]), plane)
    odd = parts_of(True, False, clock(near_mixed), far_mixed, out_weight)
    peer = swap(odd, 1)
    even = parts_of(False, False, after(near_mixed, odd), far_mixed, out_weight)
    clock.tick(even, peer)
    parts = (clock(even), peer)
    clock.tick(*send_rows(parts))
    arrived = cross(*(clock(part) for part in clock.past[:2]))
    clock.tick(*arrived, above_two, above_four)
    arrived = [clock(part) for part in arrived]
    last = cross(*pass_rows(parts, arrived))
    clock.tick(*last, down_ring[2])
    last = [clock(part) for part in last]
    middle, own_two, scale_two = on_spans(
        middle_kernel,
        own_spans(parts, arrived, last),
        (tokens, gain_two),
        (((count, model), F32), ((count, model), BF16), ((count, 1), F32)),
        "middle",
    )

    clock.tick(own_two)
    two, four = gather_pair(clock(own_two))
    clock.tick(two, four)
    six = gather_last(clock(two), clock(four))
    clock.tick(*six)
    even_two = join(clock(own_two), two, four, *six)
    odd_two = swap(even_two, 1)
    clock.tick(even_two)
    above_six = gather_last(clock(above_two), clock(above_four))
    clock.tick(mlp_weight, down_ring[2])
    down_ring.append(onward(clock(down_ring[2])))
    mlp_weight = join(clock(mlp_weight))

    def feed(normed):
        both = dot(normed, mlp_weight)
        gate, up_proj = both[:, :own_units], both[:, own_units:]
        return gate, up_proj, thin(gate * jax.nn.sigmoid(gate) * up_proj)

    even_gate, even_up, even_hidden = feed(clock(even_two))
    clock.tick(even_hidden, odd_two)
    even_above = join(clock(cotangent), above_two, above_four, *(clock(part) for part in above_six))
    odd_above = swap(even_above, 1)
    odd_gate, odd_up, odd_hidden = feed(clock(odd_two))
    clock.tick(odd_hidden, down_ring[3])
    down_weight = place_rows(finish([clock(part) for part in down_ring]), plane)
    out_odd = thin(dot(odd_hidden, down_weight))
    out_peer = swap(out_odd, 1)
    out_even = thin(dot(after(even_hidden, out_odd), down_weight))
    clock.tick(out_even, out_peer, odd_above)
    out_parts = (clock(out_even), out_peer)
    clock.tick(*send_rows(out_parts))
    out_arrived = cross(*(clock(part) for part in clock.past))
    down_sum = contract_rows(clock(even_hidden), even_above) + contract_rows(odd_hidden, odd_above)
    down_sum = thin(down_sum)
    clock.tick(down_sum)
    down_total = planes_reduce(clock(down_sum))

    def feed_back(above, gate, up_proj):
        sigmoid_gate = jax.nn.sigmoid(gate)
        hidden_grad = times_transposed(above, down_weight)
        gate_low = hidden_grad * up_proj * sigmoid_gate * (1.0 + gate * (1.0 - sigmoid_gate))
        return jnp.concatenate([thin(gate_low), thin(hidden_grad * gate * sigmoid_gate)], axis=1)

    odd_low = feed_back(clock(odd_above), odd_gate, odd_up)
    odd_part = thin(times_transposed(odd_low, mlp_weight))
    peer = swap(odd_part, 1)
    clock.tick(odd_part)
    even_low = feed_back(clock(even_above), even_gate, even_up)
    parts = (thin(times_transposed(even_low, mlp_weight)), peer)
    clock.tick(*send_rows(parts), *out_arrived)
    out_arrived = [clock(part) for part in out_arrived]
    arrived = cross(*clock.past[:2])
    mlp_sum = contract_rows(clock(even_two), even_low)
    clock.tick(*arrived, mlp_sum)
    arrived = [clock(part) for part in arrived]
    last = cross(*pass_rows(parts, arrived))
    mlp_sum = thin(mlp_sum + contract_rows(clock(odd_two), odd_low))
    clock.tick(*last, mlp_sum, down_total)
    mlp_total = planes_reduce(clock(mlp_sum))
    last = [clock(part) for part in last]
    middle_grad, branch = on_spans(
        middle_back_kernel,
        own_spans(parts, arrived, last),
        (cotangent, gain_two, middle, scale_two),
        (((count, model), F32), ((count, model), BF16)),
        "middle_back",
        60,
    )

    clock.tick(branch)
    one = swap(clock(branch), 1)
    two, four = gather_pair(clock(branch))
    near_one, far_one = join(clock(near_one_even), near_one_odd), join(clock(far_one_even), far_one_odd)
    back_weight = jnp.concatenate(
        [
            clock(attn_weight)[:, :width],
            jnp.where(core == 0, attn_weight[:, width : width + HD], attn_weight[:, width + HD :]),
        ],
        axis=1,
    )
    clock.tick(one, two, four, near_one, far_one, back_weight)
    six = gather_last(clock(two), clock(four))
    three = swap(clock(two), 1)
    clock.tick(three)

    def attention_back(kept, *blocks):
        query_low, own, other = attend_back(kept, blocks, out_weight, tables, mine, heads)
        return query_low.reshape(-1, width), own.reshape(-1, HD), swap(other.reshape(-1, HD), 1)

    near_blocks = (clock(branch), two, one, three)
    near_query, near_own, near_other = attention_back(near_kept, *near_blocks)
    clock.tick(near_query, *six)
    far_even = join(clock(four), *six)
    far_odd = swap(far_even, 1)
    near_branch = join(*near_blocks)
    clock.tick(far_odd, near_branch, near_other)
    far_branch = join(clock(far_even), far_odd)
    out_sum = contract_rows(clock(near_mixed), near_branch) + contract_rows(clock(far_mixed), far_branch)
    out_sum = thin(out_sum)
    clock.tick(out_sum, far_branch)
    far_query, far_own, far_other = attention_back(far_kept, clock(far_even), far_odd)
    near_all = jnp.concatenate([near_query, thin(near_own + near_other)], axis=1)
    clock.tick(far_query, far_other, near_all)
    far_all = jnp.concatenate([clock(far_query), thin(far_own + far_other)], axis=1)
    odd = parts_of(True, True, near_all, far_all, back_weight)
    peer = swap(odd, 1)
    even = parts_of(False, True, after(near_all, odd), far_all, back_weight)
    out_last = cross(*pass_rows(out_parts, [after(part, even) for part in out_arrived], 60))
    attn_sum = contract_rows(after(near_one, even), near_all) + contract_rows(after(far_one, even), far_all)
    clock.tick(even, peer, attn_sum)
    parts = (clock(even), peer)
    clock.tick(*send_rows(parts), mlp_total, *out_last)
    arrived = cross(*clock.past[:2])
    out_last = [clock(part) for part in out_last]
    out_total = planes_reduce(clock(out_sum))
    mlp_back = exchange(clock(mlp_total).reshape(RANKS, local, 2 * own_units))
    attn_hop = onward(clock(ring_start(attn_sum, plane, planes)))
    clock.tick(attn_hop)
    attn_hop = onward(ring_add(attn_sum, 1, clock(attn_hop), plane, planes))
    clock.tick(*arrived)
    arrived = [clock(part) for part in arrived]
    last = cross(*pass_rows(parts, arrived, 60))
    (output,) = on_spans(
        output_kernel,
        own_spans(out_parts, out_arrived, out_last),
        (clock(middle),),
        (((count, model), BF16),),
        "output",
        60,
    )
    clock.tick(attn_hop)
    attn_hop = onward(ring_add(attn_sum, 2, clock(attn_hop), plane, planes))
    for step in range(3, planes - 1):
        attn_hop = onward(ring_add(attn_sum, step, attn_hop, plane, planes))
    clock.tick(*last, mlp_back, out_total, output, attn_hop)
    mlp_back = clock(mlp_back)
    last = [clock(part) for part in last]
    attn_total = thin(ring_add(attn_sum, planes - 1, clock(attn_hop), plane, planes))
    attn_back = exchange(attn_total.reshape(RANKS, local, width + HD))
    (input_grad,) = on_spans(
        input_back_kernel,
        own_spans(parts, arrived, last),
        (after(middle_grad, attn_total), gain_one, tokens),
        (((count, model), BF16),),
        "input_back",
        60,
    )
    out_grad = lax.ppermute(after(out_total, attn_total), "dev", from_rank).astype(F32)
    clock.tick(input_grad)
    down_grad = clock(down_total).astype(F32)

    gate_grad, up_grad, mlp_gain_sum = on_rows(
        functools.partial(mlp_back_kernel, units),
        (mlp_back, w_gate, w_up),
        ((w_gate.shape, F32), (w_up.shape, F32), ((local, 1), F32)),
        "mlp_back",
    )
    query_grad, key_grad, value_grad, attn_gain_sum = on_rows(
        attn_back_kernel,
        (attn_back, w_query, w_key, w_value),
        ((w_query.shape, F32), (w_key.shape, F32), (w_value.shape, F32), ((local, 1), F32)),
        "attn_back",
    )
    return (
        output,
        input_grad,
        attn_gain_sum[:, 0] / attn_gain,
        query_grad,
        key_grad,
        value_grad,
        out_grad,
        mlp_gain_sum[:, 0] / mlp_gain,
        gate_grad,
        up_grad,
        down_grad,
    )


def solution(mesh):
    row, vec = P("dev", None), P("dev")
    return jax.shard_map(
        per_device,
        mesh=mesh,
        in_specs=(row, vec, row, row, row, row, vec, row, row, row, row),
        out_specs=(row, row, vec, row, row, row, row, vec, row, row, row),
        check_vma=False,
    )
```

```python
import functools

import jax
import jax.numpy as jnp
from jax import lax
from jax.experimental import pallas as pl
from jax.experimental.pallas import tpu as pltpu
from jax.sharding import PartitionSpec as P

HD = 64
RANKS = 8
GROUP = 4
EPS = 1e-05
THETA = 10000.0
NEG = -1e30
F32 = jnp.float32
ANY = pl.BlockSpec(memory_space=pl.ANY)
SCALAR = pl.BlockSpec(memory_space=pltpu.SMEM)
WORK = pl.CostEstimate(flops=2400000000, bytes_accessed=1, transcendentals=0)
ATTENTION_WORK = pl.CostEstimate(flops=2000000000, bytes_accessed=1, transcendentals=0)
BF16 = jnp.bfloat16


def swap(block, bit):
    n = lax.axis_size("dev")
    return lax.ppermute(block, "dev", [(i, i ^ bit) for i in range(n)])


def onward(block):
    n = lax.axis_size("dev")
    return lax.ppermute(block, "dev", [(i, (i + RANKS) % n) for i in range(n)])


def plane_groups():
    n = lax.axis_size("dev")
    return [[p * RANKS + r for r in range(RANKS)] for p in range(n // RANKS)]


def exchange(blocks):
    return lax.all_to_all(
        blocks, "dev", split_axis=0, concat_axis=0, tiled=True, axis_index_groups=plane_groups()
    )


def column_groups():
    n = lax.axis_size("dev")
    return [[p * RANKS + r for p in range(n // RANKS)] for r in range(RANKS)]


def planes_gather(block):
    return lax.all_gather(block, "dev", axis=0, tiled=True, axis_index_groups=column_groups())


def planes_reduce(terms):
    return lax.psum_scatter(
        terms, "dev", scatter_dimension=0, tiled=True, axis_index_groups=column_groups()
    )


def after(value, *earlier):
    return lax.optimization_barrier((value,) + earlier)[0]


def wide(value):
    return value.astype(F32)


def thin(value):
    return value.astype(BF16)


def copy_kernel(count, spots, first_ref, *refs):
    blocks, whole, done = refs[:count], refs[count], refs[count + 1]
    copies = []
    for i, block in enumerate(blocks):
        spot = whole.at[pl.ds(spots(i, first_ref[0]), block.shape[0])]
        copies.append(pltpu.make_async_copy(block, spot, done.at[i]))
        copies[-1].start()
    for copy in copies:
        copy.wait()


def copied(blocks, spots, first, name):
    rows = sum(block.shape[0] for block in blocks)
    return pl.pallas_call(
        functools.partial(copy_kernel, len(blocks), spots),
        in_specs=[SCALAR] + [ANY] * len(blocks),
        out_shape=jax.ShapeDtypeStruct((rows, blocks[0].shape[1]), blocks[0].dtype),
        compiler_params=pltpu.CompilerParams(vmem_limit_bytes=40 * 2**20),
        scratch_shapes=[pltpu.SemaphoreType.DMA((len(blocks),))],
        cost_estimate=WORK,
        name=name,
    )(first, *blocks)


def join(*blocks):
    starts = [0]
    for block in blocks:
        starts.append(starts[-1] + block.shape[0])
    return copied(blocks, lambda i, _: starts[i], jnp.zeros(1, jnp.int32), "join")


def gather_pair(block):
    return swap(block, 2), swap(block, 4)


def gather_last(two, four):
    half = two.shape[0] // 2
    return swap(two[:half], 4), swap(four[half:], 2)


def on_rows(function, ins, outs, name):
    return pl.pallas_call(
        function,
        out_shape=[jax.ShapeDtypeStruct(shape, dtype) for shape, dtype in outs],
        compiler_params=pltpu.CompilerParams(vmem_limit_bytes=40 * 2**20),
        cost_estimate=WORK,
        name=name,
    )(*ins)


def sliced_kernel(function, spans, whole, count, *refs):
    distant, refs = refs[:whole], refs[whole:]
    others, refs = refs[:count], refs[count:]
    outs, held, done = refs[: -len(spans) - 1], refs[-len(spans) - 1 : -1], refs[-1]
    copies = []
    for i, (which, start, rows) in enumerate(spans):
        source = distant[which].at[pl.ds(start, rows)]
        copies.append(pltpu.make_async_copy(source, held[i], done.at[i]))
        copies[-1].start()
    for copy in copies:
        copy.wait()
    function(*others, *held, *outs)


def on_spans(function, spans, others, outs, name, mebibytes=40):
    arrays = []
    for array, _, _ in spans:
        if not any(array is known for known in arrays):
            arrays.append(array)
    which = lambda array: next(i for i, known in enumerate(arrays) if array is known)
    places = tuple((which(array), start, rows) for array, start, rows in spans)
    vmem = pl.BlockSpec(memory_space=pltpu.VMEM)
    return pl.pallas_call(
        functools.partial(sliced_kernel, function, places, len(arrays), len(others)),
        in_specs=[ANY] * len(arrays) + [vmem] * len(others),
        out_shape=[jax.ShapeDtypeStruct(shape, dtype) for shape, dtype in outs],
        scratch_shapes=[pltpu.VMEM((rows, array.shape[1]), array.dtype) for array, _, rows in spans]
        + [pltpu.SemaphoreType.DMA((len(spans),))],
        compiler_params=pltpu.CompilerParams(vmem_limit_bytes=mebibytes * 2**20),
        cost_estimate=WORK,
        name=name,
    )(*arrays, *others)


def both(parts, start, rows):
    return [(part, start, rows) for part in parts]


def send_kernel(two_even, two_peer, four_even, four_peer, six_even, six_peer, to_two, to_four):
    half = two_even.shape[0]
    to_two[:half] = thin(wide(two_even[...]) + wide(two_peer[...]))
    to_four[:half] = thin(wide(four_even[...]) + wide(four_peer[...]))
    to_two[half:] = thin(wide(six_even[:half]) + wide(six_peer[:half]))
    to_four[half:] = thin(wide(six_even[half:]) + wide(six_peer[half:]))


def pass_kernel(four_even, four_peer, two_even, two_peer, from_two, from_four, to_two, to_four):
    to_four[...] = thin(wide(four_even[...]) + wide(four_peer[...]) + wide(from_two[...]))
    to_two[...] = thin(wide(two_even[...]) + wide(two_peer[...]) + wide(from_four[...]))


def send_rows(parts):
    rows, cols = parts[0].shape
    block, half = rows // 4, rows // 8
    spans = both(parts, block, half) + both(parts, 2 * block + half, half)
    spans += both(parts, 3 * block, block)
    shape = ((block, cols), BF16)
    return on_spans(send_kernel, spans, (), (shape, shape), "send_rows")


def pass_rows(parts, arrived, mebibytes=40):
    rows, cols = parts[0].shape
    block, half = rows // 4, rows // 8
    spans = both(parts, 2 * block, half) + both(parts, block + half, half)
    spans += [(part, half, half) for part in arrived]
    shape = ((half, cols), BF16)
    return on_spans(pass_kernel, spans, (), (shape, shape), "pass_rows", mebibytes)


def cross(to_two, to_four):
    return swap(to_two, 2), swap(to_four, 4)


def own_spans(parts, arrived, last):
    rows = parts[0].shape[0] // 4
    half = rows // 2
    first = [(part, 0, half) for part in arrived]
    return both(parts, 0, rows) + first + [(part, 0, half) for part in last]


def block_sum(even, peer, from_two, from_four, last_two, last_four):
    rows = last_two.shape[0]
    top, low = slice(0, rows), slice(rows, 2 * rows)
    upper = wide(even[top]) + wide(peer[top]) + wide(from_two[...]) + wide(last_four[...])
    lower = wide(even[low]) + wide(peer[low]) + wide(from_four[...]) + wide(last_two[...])
    return jnp.concatenate([upper, lower], axis=0)


def parts_kernel(odd, transposed, near, far, weight, out):
    half = near.shape[0] // 2
    span = slice(half, 2 * half) if odd else slice(0, half)
    multiply = times_transposed if transposed else dot
    out[:half] = thin(multiply(near[span], weight[...]))
    out[half:] = thin(multiply(far[span], weight[...]))


def parts_of(odd, transposed, near, far, weight):
    cols = weight.shape[0 if transposed else 1]
    return on_rows(
        functools.partial(parts_kernel, odd, transposed),
        (near, far, weight),
        (((near.shape[0], cols), BF16),),
        "odd_parts" if odd else "even_parts",
    )[0]


def mean_of(values):
    return jnp.mean(values, axis=1, keepdims=True)


def norm_kernel(gain, *refs):
    out, start = refs[-1], 0
    for block in refs[:-1]:
        values = wide(block[...])
        span = slice(start, start + block.shape[0])
        out[span] = thin(values * rms_scale(values) * gain[...])
        start += block.shape[0]


def normed(gain, *blocks):
    rows = sum(block.shape[0] for block in blocks)
    shape = (rows, blocks[0].shape[1])
    return on_rows(norm_kernel, (gain, *blocks), ((shape, BF16),), "norm")[0]


def middle_kernel(tokens, gain, *refs):
    sums, (middle_ref, normed_ref, scale_ref) = refs[:6], refs[6:]
    middle = wide(tokens[...]) + block_sum(*sums)
    scale = rms_scale(middle)
    middle_ref[...] = middle
    normed_ref[...] = thin(middle * scale * gain[...])
    scale_ref[...] = scale


def middle_back_kernel(above, gain, middle, scale, *refs):
    sums, (grad_ref, branch_ref) = refs[:6], refs[6:]
    scaled = block_sum(*sums) * gain[...]
    middle, scale = middle[...], scale[...]
    grad = wide(above[...]) + scale * scaled - middle * scale**3 * mean_of(scaled * middle)
    grad_ref[...] = grad
    branch_ref[...] = thin(grad)


def output_kernel(middle, *refs):
    refs[-1][...] = thin(middle[...] + block_sum(*refs[:6]))


def input_back_kernel(grad, gain, tokens, *refs):
    scaled = block_sum(*refs[:6]) * gain[...]
    source = wide(tokens[...])
    scale = rms_scale(source)
    whole = grad[...] + scale * scaled - source * scale**3 * mean_of(scaled * source)
    refs[-1][...] = thin(whole)


def attn_parts_kernel(query, key, value, parts):
    width = query.shape[1] // RANKS
    share = RANKS * HD // key.shape[1]
    for j in range(RANKS):
        head = slice(j // share * HD, (j // share + 1) * HD)
        parts[j, :, :width] = query[:, j * width : (j + 1) * width]
        parts[j, :, width:] = jnp.concatenate([key[:, head], value[:, head]], axis=1)


def mlp_parts_kernel(units, gate, up, parts):
    planes = gate.shape[1] // units // RANKS
    for j in range(RANKS):
        pieces = []
        for weight in (gate, up):
            for p in range(planes):
                start = (p * RANKS + j) * units
                pieces.append(weight[:, start : start + units])
        parts[j] = jnp.concatenate(pieces, axis=1)


def lane_sums(grad, weight):
    total = 0.0
    for start in range(0, grad.shape[1], 128):
        span = slice(start, start + 128)
        total = total + grad[:, span] * wide(weight[:, span])
    return jnp.sum(total, axis=1, keepdims=True)


def mlp_back_kernel(units, parts, gate, up, gate_grad, up_grad, gain_sum):
    planes = gate.shape[1] // units // RANKS
    own = planes * units
    for half, grad in enumerate((gate_grad, up_grad)):
        for p in range(planes):
            start = half * own + p * units
            pieces = [parts[j, :, start : start + units] for j in range(RANKS)]
            row = jnp.concatenate(pieces, axis=1)
            grad[:, p * RANKS * units : (p + 1) * RANKS * units] = wide(row)
    gain_sum[...] = lane_sums(gate_grad, gate) + lane_sums(up_grad, up)


def attn_back_kernel(parts, query, key, value, query_grad, key_grad, value_grad, gain_sum):
    width = query.shape[1] // RANKS
    share = RANKS * HD // key.shape[1]
    for j in range(RANKS):
        query_grad[:, j * width : (j + 1) * width] = wide(parts[j, :, :width])
    for first, grad in enumerate((key_grad, value_grad)):
        pieces = [parts[j, :, width:] for j in range(first, RANKS, share)]
        grad[...] = wide(jnp.concatenate(pieces, axis=1))
    gain_sum[...] = (
        lane_sums(query_grad, query) + lane_sums(key_grad, key) + lane_sums(value_grad, value)
    )


def place_rows(blocks, plane):
    planes, rows = len(blocks), blocks[0].shape[0]

    def spot(step, own):
        return lax.rem(own + planes - step, planes) * rows

    if rows % 16 == 0:
        aligned = lambda step, own: pl.multiple_of(spot(step, own), 16)
        return copied(blocks, aligned, plane.astype(jnp.int32).reshape(1), "place_rows")
    whole = jnp.zeros((planes * rows, blocks[0].shape[1]), blocks[0].dtype)
    for step, block in enumerate(blocks):
        whole = lax.dynamic_update_slice_in_dim(whole, block, spot(step, plane), 0)
    return whole


def place_gains(blocks, plane):
    planes, rows = len(blocks), blocks[0].shape[0]
    whole = jnp.zeros((planes * rows, blocks[0].shape[1]), blocks[0].dtype)
    for step, block in enumerate(blocks):
        place = lax.rem(plane + planes - step, planes)
        whole = lax.dynamic_update_slice_in_dim(whole, block, place * rows, 0)
    return whole


def join_gains(gains, other, bit, me):
    return jnp.where(
        me & bit,
        jnp.concatenate([other, gains], axis=1),
        jnp.concatenate([gains, other], axis=1),
    )


def ring_part(terms, step, plane, planes):
    rows = terms.shape[0] // planes
    place = lax.rem(plane + 2 * planes - 1 - step, planes)
    return lax.dynamic_slice_in_dim(terms, place * rows, rows, 0)


def ring_start(terms, plane, planes):
    return thin(ring_part(terms, 0, plane, planes))


def ring_add(terms, step, arrived, plane, planes):
    total = ring_part(terms, step, plane, planes) + wide(arrived)
    return thin(total) if step < planes - 1 else total


def dot(left, right):
    return jnp.dot(left, right, preferred_element_type=F32)


def contract_rows(left, right):
    return lax.dot_general(left, right, (((0,), (0,)), ((), ())), preferred_element_type=F32)


def times_transposed(left, right):
    return lax.dot_general(left, right, (((1,), (1,)), ((), ())), preferred_element_type=F32)


def rms_scale(values):
    return lax.rsqrt(jnp.mean(values * values, axis=1, keepdims=True) + EPS)


def rope_tables(length):
    lanes = jnp.arange(2 * HD)
    frequency = THETA ** (-((lanes % (HD // 2)).astype(F32) * 2.0 / HD))
    angles = jnp.arange(length).astype(F32)[:, None] * frequency[None, :]
    sign = jnp.where(lanes % HD < HD // 2, -1.0, 1.0)
    return jnp.cos(angles), jnp.sin(angles) * sign[None, :]


def slot_of(place, mine):
    turn = place ^ mine
    return ((turn & 1) << 1) | (turn >> 1)


def spot_of(place, mine, rows):
    return pl.ds(pl.multiple_of(slot_of(place, mine) * rows, rows), rows)


def partner(values):
    lane = lax.broadcasted_iota(jnp.int32, values.shape, 1)
    ahead = pltpu.roll(values, 2 * HD - HD // 2, 1)
    behind = pltpu.roll(values, HD // 2, 1)
    return jnp.where(lane % HD < HD // 2, ahead, behind)


def fetch(blocks, whole, done):
    copies, start = [], 0
    for i, block in enumerate(blocks):
        spot = whole.at[pl.ds(start, block.shape[0])]
        copies.append(pltpu.make_async_copy(block, spot, done.at[i]))
        copies[-1].start()
        start += block.shape[0]
    for copy in copies:
        copy.wait()


def heads_beside(stacked, heads):
    return jnp.concatenate([stacked[h * HD : (h + 1) * HD] for h in range(heads)], axis=1)


def heads_below(beside, heads):
    rows = beside.shape[1] // heads
    return jnp.concatenate([beside[:, h * rows : (h + 1) * rows] for h in range(heads)], axis=0)


def causal(rows, heads):
    key = lax.broadcasted_iota(jnp.int32, (rows, heads * rows), 0)
    query = lax.broadcasted_iota(jnp.int32, (rows, heads * rows), 1)
    return key <= query % rows


def forward_kernel(heads, rows, count, m_ref, *refs):
    blocks, refs = refs[:count], refs[count:]
    weight_ref, cos_ref, sin_ref, mixed_ref, qt_ref, kv_ref, lse_ref, normed_ref, done = refs
    fetch(blocks, normed_ref, done)
    mine = m_ref[0]
    width = heads * HD
    is_key = lax.broadcasted_iota(jnp.int32, (rows, 2 * HD), 1) < HD
    ok = causal(rows, heads)
    for p in range(GROUP):
        span = slice(p * rows, (p + 1) * rows)
        qkv = dot(normed_ref[spot_of(p, mine, rows), :], weight_ref[...])
        cosine, sine = cos_ref[span, :], sin_ref[span, :]
        turned = []
        for start in range(0, width, 2 * HD):
            part = qkv[:, start : start + 2 * HD]
            turned.append(part * cosine + partner(part) * sine)
        query = jnp.concatenate(turned, axis=1) * HD ** (-0.5)
        qt_ref[0, p] = heads_beside(query.T, heads).astype(BF16)
        part = qkv[:, width : width + 2 * HD]
        kv_ref[0, span, :] = jnp.where(
            is_key, part * cosine + partner(part) * sine, part
        ).astype(BF16)
    kv = kv_ref[0]
    vt = kv.astype(F32).T.astype(BF16)[HD:, :]
    keys = kv[:, :HD]
    for p in range(GROUP):
        span = slice(p * rows, (p + 1) * rows)
        query = qt_ref[0, p]
        last = jnp.where(ok, dot(keys[span], query), NEG)
        top = jnp.max(last, axis=0, keepdims=True)
        if p:
            first = dot(keys[: p * rows], query)
            top = jnp.maximum(top, jnp.max(first, axis=0, keepdims=True))
        last = jnp.exp(last - top)
        total = jnp.sum(last, axis=0, keepdims=True)
        if p:
            first = jnp.exp(first - top)
            total = total + jnp.sum(first, axis=0, keepdims=True)
        share = 1.0 / total
        out = dot(vt[:, span], (last * share).astype(BF16))
        if p:
            out = out + dot(vt[:, : p * rows], (first * share).astype(BF16))
        mixed_ref[0, slot_of(p, mine)] = heads_below(out, heads).T.astype(BF16)
        lse_ref[0, p] = top + jnp.log(total)


def backward_kernel(heads, rows, count, m_ref, *refs):
    blocks, refs = refs[:count], refs[count:]
    qt_ref, kv_ref, lse_ref, out_ref, cos_ref, sin_ref, *refs = refs
    dq_ref, kept_ref, sent_ref, dk_sum, dv_sum, branch_ref, done = refs
    fetch(blocks, branch_ref, done)
    mine = m_ref[0]
    width = heads * HD
    kv = kv_ref[0]
    kt = kv.astype(F32).T.astype(BF16)[:HD, :]
    keys = kv[:, :HD]
    values = pltpu.roll(kv.astype(F32), HD, 1).astype(BF16)[:, :HD]
    ok = causal(rows, heads)
    for p in reversed(range(GROUP)):
        span = slice(p * rows, (p + 1) * rows)
        reach = (p + 1) * rows
        grad = thin(times_transposed(out_ref[...], branch_ref[spot_of(p, mine, rows), :]))
        above = heads_beside(grad, heads)
        query = qt_ref[0, p]
        scores = dot(keys[:reach], query)
        last = jnp.where(ok, scores[p * rows :], NEG)
        scores = jnp.concatenate([scores[: p * rows], last], axis=0) if p else last
        probs = jnp.exp(scores - lse_ref[0, p])
        probs_grad = dot(values[:reach], above)
        delta = jnp.sum(probs * probs_grad, axis=0, keepdims=True)
        score_low = (probs * (probs_grad - delta)).astype(BF16)
        dk = times_transposed(score_low, query)
        dv = times_transposed(probs.astype(BF16), above)
        if p == GROUP - 1:
            dk_sum[...] = dk
            dv_sum[...] = dv
        else:
            dk_sum[:reach, :] += dk
            dv_sum[:reach, :] += dv
        dq = heads_below(dot(kt[:, :reach], score_low), heads).T * HD ** (-0.5)
        cosine, sine = cos_ref[span, :], sin_ref[span, :]
        turned = []
        for start in range(0, width, 2 * HD):
            part = dq[:, start : start + 2 * HD]
            turned.append(part * cosine - partner(part) * sine)
        dq_ref[0, slot_of(p, mine)] = jnp.concatenate(turned, axis=1).astype(BF16)
    is_key = lax.broadcasted_iota(jnp.int32, (rows, 2 * HD), 1) < HD
    for p in range(GROUP):
        span = slice(p * rows, (p + 1) * rows)
        part = jnp.concatenate([dk_sum[span, :], dv_sum[span, :]], axis=1)
        cosine, sine = cos_ref[span, :], sin_ref[span, :]
        part = jnp.where(is_key, part * cosine - partner(part) * sine, part)
        turned = pltpu.roll(part, HD, 1)
        even = (mine & 1) == 0
        kept_ref[0, slot_of(p, mine)] = jnp.where(even, part, turned)[:, :HD]
        sent_ref[0, slot_of(p, mine ^ 1)] = jnp.where(even, turned, part)[:, :HD]


def same_spec(shape):
    zeros = (0,) * len(shape)
    return pl.BlockSpec(shape, lambda i, m: zeros)


def attention_call(kernel, mine, blocks, others, shapes, scratch, name):
    length = sum(block.shape[0] for block in blocks)
    return pl.pallas_call(
        kernel,
        grid_spec=pltpu.PrefetchScalarGridSpec(
            num_scalar_prefetch=1,
            grid=(1,),
            in_specs=[ANY] * len(blocks) + [same_spec(v.shape) for v in others],
            out_specs=[same_spec(shape) for shape, _ in shapes],
            scratch_shapes=scratch
            + [
                pltpu.VMEM((length, blocks[0].shape[1]), BF16),
                pltpu.SemaphoreType.DMA((len(blocks),)),
            ],
        ),
        out_shape=[jax.ShapeDtypeStruct(shape, dtype) for shape, dtype in shapes],
        compiler_params=pltpu.CompilerParams(vmem_limit_bytes=48 * 2**20),
        cost_estimate=ATTENTION_WORK,
        name=name,
    )(mine, *blocks, *others)


def attend(blocks, weight, tables, mine, heads):
    length = tables[0].shape[0]
    rows, width = length // GROUP, heads * HD
    shapes = (
        ((1, GROUP, rows, width), BF16),
        ((1, GROUP, HD, heads * rows), BF16),
        ((1, length, 2 * HD), BF16),
        ((1, GROUP, 1, heads * rows), F32),
    )
    kernel = functools.partial(forward_kernel, heads, rows, len(blocks))
    return attention_call(kernel, mine, blocks, (weight, *tables), shapes, [], "attend")


def attend_back(kept, blocks, out_weight, tables, mine, heads):
    length = tables[0].shape[0]
    rows, width = length // GROUP, heads * HD
    half = ((1, GROUP, rows, HD), F32)
    shapes = (((1, GROUP, rows, width), BF16), half, half)
    scratch = [pltpu.VMEM((length, HD), F32), pltpu.VMEM((length, HD), F32)]
    kernel = functools.partial(backward_kernel, heads, rows, len(blocks))
    others = (*kept, out_weight, *tables)
    return attention_call(kernel, mine, blocks, others, shapes, scratch, "attend_back")


class Clock:
    def __init__(self):
        self.past = ()

    def __call__(self, value):
        return after(value, *self.past) if self.past else value

    def tick(self, *values):
        self.past = values


def per_device(
    tokens, attn_gain, w_query, w_key, w_value, w_out, mlp_gain, w_gate, w_up, w_down, cotangent
):
    n = lax.axis_size("dev")
    planes = n // RANKS
    me = lax.axis_index("dev")
    plane, rank = me // RANKS, lax.rem(me, RANKS)
    core = lax.rem(me, 2)
    mine = lax.rem(me, GROUP).astype(jnp.int32).reshape(1)
    count, model = tokens.shape
    local = w_query.shape[0]
    heads = w_query.shape[1] // HD // RANKS
    kv_heads = w_key.shape[1] // HD
    width = heads * HD
    units = w_gate.shape[1] // n
    own_units = units * planes
    seqs = RANKS // GROUP
    share = RANKS // kv_heads

    to_rank = [(i, (i % planes) * RANKS + i // planes) for i in range(n)]
    from_rank = [(j, i) for i, j in to_rank]
    attn_cols = width + 2 * HD
    clock = Clock()

    def finish(ring, *tail):
        while len(ring) < planes:
            ring = ring + [onward(ring[-1])]
        return ring

    (attn_parts,) = on_rows(
        attn_parts_kernel,
        (w_query, w_key, w_value),
        (((RANKS, local, attn_cols), BF16),),
        "attn_parts",
    )
    attn_own = exchange(attn_parts).reshape(RANKS * local, attn_cols)
    gains = after(jnp.stack([attn_gain, mlp_gain]), attn_parts)
    gain_ring = [gains]
    for step in range(1, planes):
        route = [(i, (i + RANKS * step) % n) for i in range(n)]
        gain_ring.append(lax.ppermute(gains, "dev", route))
    gains = place_gains(gain_ring, plane)
    for bit in (1, 2, 4):
        gains = join_gains(gains, swap(gains, bit), bit, me)
    gain_rows = gains.reshape(planes, 2, -1).transpose(1, 0, 2)
    gain_one, gain_two = jnp.split(gain_rows.reshape(2, model).astype(F32), 2)
    out_ring = [lax.ppermute(after(w_out, attn_parts), "dev", to_rank)]
    (mlp_parts,) = on_rows(
        functools.partial(mlp_parts_kernel, units),
        (w_gate, w_up),
        (((RANKS, local, 2 * own_units), BF16),),
        "mlp_parts",
    )
    tables = rope_tables(GROUP * count)
    clock.tick(gain_one, gain_two, mlp_parts, *tables)
    attn_own = clock(attn_own)
    clock.tick(attn_own, out_ring[0])
    two, four = gather_pair(clock(tokens))
    attn_ring = [attn_own, onward(clock(attn_own))]
    clock.tick(attn_ring[1])
    attn_ring.append(onward(clock(attn_ring[1])))
    out_ring.append(onward(clock(out_ring[0])))
    clock.tick(two, four, attn_ring[2], out_ring[1])
    six = gather_last(clock(two), clock(four))
    attn_ring.append(onward(clock(attn_ring[2])))
    near_even = normed(gain_one, clock(tokens), two)
    near_odd = swap(near_even, 1)
    out_ring.append(onward(clock(out_ring[1])))
    clock.tick(near_odd, attn_ring[3], out_ring[2], *six)
    mlp_own = exchange(clock(mlp_parts)).reshape(RANKS * local, 2 * own_units)
    attn_weight = place_rows(finish([clock(block) for block in attn_ring]), plane)
    far_even = normed(gain_one, clock(four), *six)
    far_odd = swap(far_even, 1)
    clock.tick(attn_weight, far_even)
    out_ring.append(onward(clock(out_ring[2])))
    down_ring = [w_down, onward(clock(w_down))]

    near_one_even, near_one_odd, far_one_even, far_one_odd = near_even, near_odd, far_even, far_odd
    near_mixed, *near_kept = attend((clock(near_even), near_odd), attn_weight, tables, mine, heads)
    clock.tick(near_mixed, far_odd, mlp_own, down_ring[1])
    above_two, above_four = gather_pair(clock(cotangent))
    down_ring.append(onward(clock(down_ring[1])))
    mlp_weight = planes_gather(clock(mlp_own))
    far_mixed, *far_kept = attend((clock(far_even), far_odd), attn_weight, tables, mine, heads)
    far_mixed, near_mixed = far_mixed.reshape(-1, width), near_mixed.reshape(-1, width)
    clock.tick(far_mixed, out_ring[3])
    out_weight = place_rows(finish([clock(block) for block in out_ring]), plane)
    odd = parts_of(True, False, clock(near_mixed), far_mixed, out_weight)
    peer = swap(odd, 1)
    even = parts_of(False, False, after(near_mixed, odd), far_mixed, out_weight)
    clock.tick(even, peer)
    parts = (clock(even), peer)
    clock.tick(*send_rows(parts))
    arrived = cross(*(clock(part) for part in clock.past[:2]))
    clock.tick(*arrived, above_two, above_four)
    arrived = [clock(part) for part in arrived]
    last = cross(*pass_rows(parts, arrived))
    clock.tick(*last, down_ring[2])
    last = [clock(part) for part in last]
    middle, own_two, scale_two = on_spans(
        middle_kernel,
        own_spans(parts, arrived, last),
        (tokens, gain_two),
        (((count, model), F32), ((count, model), BF16), ((count, 1), F32)),
        "middle",
    )

    clock.tick(own_two)
    two, four = gather_pair(clock(own_two))
    clock.tick(two, four)
    six = gather_last(clock(two), clock(four))
    clock.tick(*six)
    even_two = join(clock(own_two), two, four, *six)
    odd_two = swap(even_two, 1)
    clock.tick(even_two)
    above_six = gather_last(clock(above_two), clock(above_four))
    clock.tick(mlp_weight, down_ring[2])
    down_ring.append(onward(clock(down_ring[2])))
    mlp_weight = join(clock(mlp_weight))

    def feed(normed):
        both = dot(normed, mlp_weight)
        gate, up_proj = both[:, :own_units], both[:, own_units:]
        return gate, up_proj, thin(gate * jax.nn.sigmoid(gate) * up_proj)

    even_gate, even_up, even_hidden = feed(clock(even_two))
    clock.tick(even_hidden, odd_two)
    even_above = join(clock(cotangent), above_two, above_four, *(clock(part) for part in above_six))
    odd_above = swap(even_above, 1)
    odd_gate, odd_up, odd_hidden = feed(clock(odd_two))
    clock.tick(odd_hidden, down_ring[3])
    down_weight = place_rows(finish([clock(part) for part in down_ring]), plane)
    out_odd = thin(dot(odd_hidden, down_weight))
    out_peer = swap(out_odd, 1)
    out_even = thin(dot(after(even_hidden, out_odd), down_weight))
    clock.tick(out_even, out_peer, odd_above)
    out_parts = (clock(out_even), out_peer)
    clock.tick(*send_rows(out_parts))
    out_arrived = cross(*(clock(part) for part in clock.past))
    down_sum = contract_rows(clock(even_hidden), even_above) + contract_rows(odd_hidden, odd_above)
    down_sum = thin(down_sum)
    clock.tick(down_sum)
    down_total = planes_reduce(clock(down_sum))

    def feed_back(above, gate, up_proj):
        sigmoid_gate = jax.nn.sigmoid(gate)
        hidden_grad = times_transposed(above, down_weight)
        gate_low = hidden_grad * up_proj * sigmoid_gate * (1.0 + gate * (1.0 - sigmoid_gate))
        return jnp.concatenate([thin(gate_low), thin(hidden_grad * gate * sigmoid_gate)], axis=1)

    odd_low = feed_back(clock(odd_above), odd_gate, odd_up)
    odd_part = thin(times_transposed(odd_low, mlp_weight))
    peer = swap(odd_part, 1)
    clock.tick(odd_part)
    even_low = feed_back(clock(even_above), even_gate, even_up)
    parts = (thin(times_transposed(even_low, mlp_weight)), peer)
    clock.tick(*send_rows(parts), *out_arrived)
    out_arrived = [clock(part) for part in out_arrived]
    arrived = cross(*clock.past[:2])
    mlp_sum = contract_rows(clock(even_two), even_low)
    clock.tick(*arrived, mlp_sum)
    arrived = [clock(part) for part in arrived]
    last = cross(*pass_rows(parts, arrived))
    mlp_sum = thin(mlp_sum + contract_rows(clock(odd_two), odd_low))
    clock.tick(*last, mlp_sum, down_total)
    mlp_total = planes_reduce(clock(mlp_sum))
    last = [clock(part) for part in last]
    middle_grad, branch = on_spans(
        middle_back_kernel,
        own_spans(parts, arrived, last),
        (cotangent, gain_two, middle, scale_two),
        (((count, model), F32), ((count, model), BF16)),
        "middle_back",
        60,
    )

    clock.tick(branch)
    one = swap(clock(branch), 1)
    two, four = gather_pair(clock(branch))
    near_one, far_one = join(clock(near_one_even), near_one_odd), join(clock(far_one_even), far_one_odd)
    back_weight = jnp.concatenate(
        [
            clock(attn_weight)[:, :width],
            jnp.where(core == 0, attn_weight[:, width : width + HD], attn_weight[:, width + HD :]),
        ],
        axis=1,
    )
    clock.tick(one, two, four, near_one, far_one, back_weight)
    six = gather_last(clock(two), clock(four))
    three = swap(clock(two), 1)
    clock.tick(three)

    def attention_back(kept, *blocks):
        query_low, own, other = attend_back(kept, blocks, out_weight, tables, mine, heads)
        return query_low.reshape(-1, width), own.reshape(-1, HD), swap(other.reshape(-1, HD), 1)

    near_blocks = (clock(branch), two, one, three)
    near_query, near_own, near_other = attention_back(near_kept, *near_blocks)
    clock.tick(near_query, *six)
    far_even = join(clock(four), *six)
    far_odd = swap(far_even, 1)
    near_branch = join(*near_blocks)
    clock.tick(far_odd, near_branch, near_other)
    far_branch = join(clock(far_even), far_odd)
    out_sum = contract_rows(clock(near_mixed), near_branch) + contract_rows(clock(far_mixed), far_branch)
    out_sum = thin(out_sum)
    clock.tick(out_sum, far_branch)
    far_query, far_own, far_other = attention_back(far_kept, clock(far_even), far_odd)
    near_all = jnp.concatenate([near_query, thin(near_own + near_other)], axis=1)
    clock.tick(far_query, far_other, near_all)
    far_all = jnp.concatenate([clock(far_query), thin(far_own + far_other)], axis=1)
    odd = parts_of(True, True, near_all, far_all, back_weight)
    peer = swap(odd, 1)
    even = parts_of(False, True, after(near_all, odd), far_all, back_weight)
    out_last = cross(*pass_rows(out_parts, [after(part, even) for part in out_arrived], 60))
    attn_sum = contract_rows(after(near_one, even), near_all) + contract_rows(after(far_one, even), far_all)
    clock.tick(even, peer, attn_sum)
    parts = (clock(even), peer)
    clock.tick(*send_rows(parts), mlp_total, *out_last)
    arrived = cross(*clock.past[:2])
    out_last = [clock(part) for part in out_last]
    out_total = planes_reduce(clock(out_sum))
    mlp_back = exchange(clock(mlp_total).reshape(RANKS, local, 2 * own_units))
    attn_hop = onward(clock(ring_start(attn_sum, plane, planes)))
    clock.tick(attn_hop)
    attn_hop = onward(ring_add(attn_sum, 1, clock(attn_hop), plane, planes))
    clock.tick(*arrived)
    arrived = [clock(part) for part in arrived]
    last = cross(*pass_rows(parts, arrived, 60))
    (output,) = on_spans(
        output_kernel,
        own_spans(out_parts, out_arrived, out_last),
        (clock(middle),),
        (((count, model), BF16),),
        "output",
        60,
    )
    clock.tick(attn_hop)
    attn_hop = onward(ring_add(attn_sum, 2, clock(attn_hop), plane, planes))
    for step in range(3, planes - 1):
        attn_hop = onward(ring_add(attn_sum, step, attn_hop, plane, planes))
    clock.tick(*last, mlp_back, out_total, output, attn_hop)
    mlp_back = clock(mlp_back)
    last = [clock(part) for part in last]
    attn_total = thin(ring_add(attn_sum, planes - 1, clock(attn_hop), plane, planes))
    attn_back = exchange(attn_total.reshape(RANKS, local, width + HD))
    (input_grad,) = on_spans(
        input_back_kernel,
        own_spans(parts, arrived, last),
        (after(middle_grad, attn_total), gain_one, tokens),
        (((count, model), BF16),),
        "input_back",
        60,
    )
    out_grad = lax.ppermute(after(out_total, attn_total), "dev", from_rank).astype(F32)
    clock.tick(input_grad)
    down_grad = clock(down_total).astype(F32)

    gate_grad, up_grad, mlp_gain_sum = on_rows(
        functools.partial(mlp_back_kernel, units),
        (mlp_back, w_gate, w_up),
        ((w_gate.shape, F32), (w_up.shape, F32), ((local, 1), F32)),
        "mlp_back",
    )
    query_grad, key_grad, value_grad, attn_gain_sum = on_rows(
        attn_back_kernel,
        (attn_back, w_query, w_key, w_value),
        ((w_query.shape, F32), (w_key.shape, F32), (w_value.shape, F32), ((local, 1), F32)),
        "attn_back",
    )
    return (
        output,
        input_grad,
        attn_gain_sum[:, 0] / attn_gain,
        query_grad,
        key_grad,
        value_grad,
        out_grad,
        mlp_gain_sum[:, 0] / mlp_gain,
        gate_grad,
        up_grad,
        down_grad,
    )


def solution(mesh):
    row, vec = P("dev", None), P("dev")
    return jax.shard_map(
        per_device,
        mesh=mesh,
        in_specs=(row, vec, row, row, row, row, vec, row, row, row, row),
        out_specs=(row, row, vec, row, row, row, row, vec, row, row, row),
        check_vma=False,
    )
```
